512 devices in a mesh: tiles: 32 (over z, core), sub: 16 (over y, x).
Axes of the slice: x: 4, y: 4, z: 16, core: 2. Of those that a mesh axis runs over, the one named last changes fastest.
Arguments:
- strips: bfloat16 [64, 4, 128, 32, 256], P('tiles', None, 'sub'), may hold values from -16 to 16
- pair_tiles: int32 [108, 2], replicated, may hold values from 0 to 63, as said below
- pair_owner: int32 [108], replicated, may hold values from 0 to 31, as said below
- pair_offset: int32 [108, 3], replicated, may hold values from -5 to 5
Outputs:
- windows: float32 [192, 729], P('tiles')
- normal_matrix: float32 [64, 64], replicated
- normal_rhs: float32 [64, 3], replicated
The draws below stay inside these ranges and needn't reach their ends.
Inputs may be any that keep to these rules, and one draw needn't show every extreme that they name: `pair_tiles`: tiles are numbered row by row in rows of 4; each row names a = the left or upper tile and b = a + 1 in the same row or b = a + 4; every adjacent pair is listed exactly once. `pair_owner`: tile t lies on index t // 2 of tiles; the owner of a pair is the index that holds tile a or the index that holds tile b; no index owns more than 6 pairs, and some index owns exactly 6.
All inputs are finite; a program needn't handle non-finite values.
Results may differ from the reference program's by a relative error of at most 0.0003.
Values may be sent and summed in bfloat16 or wider, within the bound.
No kernel may reach another device: no remote copies, remote signals or barrier semaphores. Data moves between devices by JAX's collectives and lax.ppermute only.
A program may use at most 64 MiB of HBM per device.

```python
import jax
import jax.numpy as jnp
from jax import lax

ACROSS = 32
ALONG = 256
DEPTH = 128
REACH = 4
TILE_DEV = 2
WIN = 9
TILES = 64
ROW = 4
ROWS = 16
PAIRS = 108
CAP = 6
N_TILES = 32


def seam_table(key):
    across_count = (ROW - 1) * ROWS
    position = jnp.arange(PAIRS, dtype=jnp.int32)
    across_seam = position < across_count
    first_tile = jnp.where(across_seam, position // (ROW - 1) * ROW + position % (ROW - 1), position - across_count)
    second_tile = jnp.where(across_seam, first_tile + 1, first_tile + ROW)
    true_shift = jax.random.randint(jax.random.fold_in(key, 7), (PAIRS, 3), -3, 4)
    shuffle = jax.random.permutation(jax.random.fold_in(key, 8), PAIRS)
    return (first_tile, second_tile, true_shift, shuffle)


def draw_pair_tiles(key, part):
    first_tile, second_tile, true_shift, shuffle = seam_table(key)
    return jnp.stack([first_tile[shuffle], second_tile[shuffle]], axis=1).astype(jnp.int32)


def draw_pair_offset(key, part):
    first_tile, second_tile, true_shift, shuffle = seam_table(key)
    key = jax.random.fold_in(key, 12)
    errors = jax.random.randint(key, (PAIRS, 3), -2, 3)
    return (true_shift[shuffle] + errors).astype(jnp.int32)


def draw_pair_owner(key, part):
    first_tile, second_tile, true_shift, shuffle = seam_table(key)
    key = jax.random.fold_in(key, 13)
    devices = TILES // TILE_DEV
    priority = jax.random.permutation(jax.random.fold_in(key, 1), devices)
    favourite = jax.random.randint(jax.random.fold_in(key, 2), (), 3, devices - 3)
    priority = jnp.where(jnp.arange(devices) == favourite, devices, priority)
    tile_a = first_tile[shuffle]
    tile_b = second_tile[shuffle]
    owner_first = tile_a // TILE_DEV
    owner_second = tile_b // TILE_DEV
    owner = jnp.where(priority[owner_first] >= priority[owner_second], owner_first, owner_second)
    owner = jnp.where((tile_a == TILE_DEV - 1) & (tile_b == TILE_DEV), 0, owner)
    owner = jnp.where((tile_a == TILES - TILE_DEV - 1) & (tile_b == TILES - TILE_DEV), devices - 1, owner)
    owner = jnp.where((tile_a == 0) & (tile_b == ROW), 2, owner)
    owner = jnp.where((tile_a == 1) & (tile_b == ROW + 1), 0, owner)
    owner = jnp.where((tile_a == TILES - ROW - TILE_DEV) & (tile_b == TILES - TILE_DEV), devices - 1, owner)
    owner = jnp.where((tile_a == TILES - ROW - TILE_DEV + 1) & (tile_b == TILES - TILE_DEV + 1), devices - 3, owner)
    return owner.astype(jnp.int32)


def draw_strips(key, part):
    first_tile, second_tile, true_shift, shuffle = seam_table(key)
    key = jax.random.fold_in(key, 14)
    bright_low, bright_high = (0.3, 3.0)
    base_key = jax.random.fold_in(key, 1)
    speckle_key = jax.random.fold_in(key, 2)
    brightness = jnp.exp(jax.random.uniform(jax.random.fold_in(key, 3), (TILES,), minval=jnp.log(bright_low), maxval=jnp.log(bright_high)))
    across_count = (ROW - 1) * ROWS
    extent = (DEPTH, ACROSS, ALONG)

    def sample(field_key):
        gauss = jax.random.normal(jax.random.fold_in(field_key, 2), extent)
        return gauss

    def element(number):
        tile_number = number // 4
        side_code = number % 4
        row_number = tile_number // ROW
        col_number = tile_number % ROW
        has_seam = jnp.select([side_code == 0, side_code == 1, side_code == 2], [col_number > 0, col_number < ROW - 1, row_number > 0], row_number < ROWS - 1)
        seam_id = jnp.select([side_code == 0, side_code == 1, side_code == 2], [row_number * (ROW - 1) + col_number - 1, row_number * (ROW - 1) + col_number, across_count + (row_number - 1) * ROW + col_number], across_count + row_number * ROW + col_number)
        seam_id = jnp.clip(seam_id, 0, PAIRS - 1)
        shared_field = sample(jax.random.fold_in(base_key, seam_id))
        speckle = sample(jax.random.fold_in(speckle_key, number))
        rolled = jnp.roll(shared_field, (-true_shift[seam_id, 0], -true_shift[seam_id, 1], -true_shift[seam_id, 2]), axis=(0, 1, 2))
        content = jnp.where(side_code % 2 == 0, rolled, shared_field)
        voxels = jnp.where(has_seam, 0.8 * content + 0.6 * speckle, speckle) * brightness[tile_number]
        return jnp.clip(voxels, -16.0, 16.0).astype(jnp.bfloat16)
    stacked = lax.map(element, jnp.arange(TILES * 4, dtype=jnp.int32))
    return stacked.reshape(TILES, 4, DEPTH, ACROSS, ALONG)


def setup_inputs(seed: int = 0) -> dict:
    streams_of = jax.random.split(jax.random.key(seed), 5)
    strips = draw_strips(jax.random.fold_in(streams_of[4], 71), 0)
    pair_tiles = draw_pair_tiles(jax.random.fold_in(streams_of[4], 71), 0)
    pair_owner = draw_pair_owner(jax.random.fold_in(streams_of[4], 71), 0)
    pair_offset = draw_pair_offset(jax.random.fold_in(streams_of[4], 71), 0)
    return {"strips": strips, "pair_tiles": pair_tiles, "pair_owner": pair_owner, "pair_offset": pair_offset}


EPSILON = 1e-06
FLOOR_SHARE = 0.05

def pair_window(first_strip, second_strip, offset):
    voxel_count = DEPTH * ACROSS * ALONG
    first_spec = jnp.fft.fftn(first_strip.astype(jnp.float32))
    second_spec = jnp.fft.fftn(second_strip.astype(jnp.float32))
    cross_spec = first_spec * jnp.conj(second_spec)
    magnitude = jnp.sqrt(jnp.real(cross_spec) ** 2 + jnp.imag(cross_spec) ** 2 + (FLOOR_SHARE * voxel_count) ** 2)
    correlation = jnp.real(jnp.fft.ifftn(cross_spec / magnitude))
    window_steps = jnp.arange(WIN, dtype=jnp.int32) - REACH
    depth_pos = (offset[0] + window_steps) % DEPTH
    across_pos = (offset[1] + window_steps) % ACROSS
    along_pos = (offset[2] + window_steps) % ALONG
    picked = correlation[depth_pos[:, None, None], across_pos[None, :, None], along_pos[None, None, :]]
    return picked.reshape(-1)

def reference(strips, pair_tiles, pair_owner, pair_offset):
    first_tile = pair_tiles[:, 0]
    second_tile = pair_tiles[:, 1]
    across_seam = second_tile - first_tile == 1
    side_first = jnp.where(across_seam, 1, 3).astype(jnp.int32)
    side_second = jnp.where(across_seam, 0, 2).astype(jnp.int32)

    def one_pair(position):
        return pair_window(strips[first_tile[position], side_first[position]], strips[second_tile[position], side_second[position]], pair_offset[position])
    windows = lax.map(one_pair, jnp.arange(PAIRS, dtype=jnp.int32))
    earlier = jnp.arange(PAIRS)[:, None] > jnp.arange(PAIRS)[None, :]
    ordinal = lax.optimization_barrier(jnp.sum(earlier & (pair_owner[:, None] == pair_owner[None, :]), axis=1)).astype(jnp.int32)
    row_slot = pair_owner * CAP + ordinal
    window_out = jnp.zeros((N_TILES * CAP, WIN * WIN * WIN), jnp.float32).at[row_slot].set(windows)
    win_index = jnp.arange(WIN * WIN * WIN, dtype=jnp.int32)
    displace = jnp.stack([win_index // (WIN * WIN), win_index // WIN % WIN, win_index % WIN], axis=1) - REACH
    squares = windows * windows
    energy = lax.optimization_barrier(jnp.sum(squares, axis=1))
    estimate = pair_offset.astype(jnp.float32) + jnp.dot(squares, displace.astype(jnp.float32), precision=lax.Precision.HIGHEST) / (energy + EPSILON)[:, None]
    tile_ids = jnp.arange(TILES, dtype=jnp.int32)
    incidence = (first_tile[:, None] == tile_ids[None, :]).astype(jnp.float32) - (second_tile[:, None] == tile_ids[None, :]).astype(jnp.float32)
    weighted = incidence * energy[:, None]
    normal_matrix = jnp.dot(weighted.T, incidence, precision=lax.Precision.HIGHEST)
    normal_rhs = jnp.dot(weighted.T, estimate, precision=lax.Precision.HIGHEST)
    return (window_out, normal_matrix, normal_rhs)
```

```python
import jax
import jax.numpy as jnp
import ml_dtypes
import numpy as np
from jax import lax
from jax.experimental import pallas as pl
from jax.experimental.pallas import tpu as pltpu
from jax.sharding import Mesh, PartitionSpec as P

REACH = 4
WIN = 9
EPSILON = 1e-06
FLOOR_SHARE = 0.05
ROW = 4
PLANES = 16
SUBS = 16
DEPTH, ACROSS, ALONG = 128, 32, 256
LOCAL = DEPTH // SUBS
HALF = ALONG // 2
VOXELS = DEPTH * ACROSS * ALONG
MAX_OFF = 5
OFFS = 2 * MAX_OFF + 1
SLOTS = 7
BF = jnp.bfloat16
F32 = jnp.float32


def split_np(table):
    high = table.astype(ml_dtypes.bfloat16)
    low = (table - high.astype(np.float64)).astype(ml_dtypes.bfloat16)
    return high, low


def angles(rows, cols, length):
    return (np.outer(rows, cols) % length) * (2.0 * np.pi / length)


def across_freq(half, sub):
    if half == 0:
        return sub
    return ACROSS // 2 if sub == 0 else ACROSS - sub


def across_table():
    table = np.zeros((2, 2, SUBS, LOCAL, LOCAL, ACROSS))
    for half in range(2):
        for sub in range(SUBS):
            theta = angles([across_freq(half, sub)], np.arange(ACROSS), ACROSS)[0]
            for plane in range(LOCAL):
                table[half, 0, sub, plane, plane] = np.cos(theta)
                table[half, 1, sub, plane, plane] = -np.sin(theta)
    return table.reshape(2, 2 * SUBS * LOCAL, LOCAL * ACROSS)


def along_table():
    table = np.zeros((2, 2, ALONG, 2, HALF))
    for half in range(2):
        theta = angles(np.arange(ALONG), np.arange(HALF) + half, ALONG)
        table[half, 0, :, 0] = np.cos(theta)
        table[half, 0, :, 1] = -np.sin(theta)
        table[half, 1, :, 0] = np.sin(theta)
        table[half, 1, :, 1] = np.cos(theta)
    return table.reshape(2, 2 * ALONG, 2 * HALF)


def extra_table():
    table = np.zeros((2, ALONG, HALF))
    table[0, :, 0] = np.where(np.arange(ALONG) % 2 == 0, 1.0, -1.0)
    table[1, :, HALF - 1] = 1.0
    return table


def depth_table():
    theta = angles(np.arange(DEPTH), np.arange(DEPTH), DEPTH).reshape(DEPTH, SUBS, LOCAL)
    table = np.zeros((2, 2, DEPTH, SUBS, 2, LOCAL))
    for half in range(2):
        table[0, half, :, :, half, :] = np.cos(theta)
        table[1, half, :, :, half, :] = np.sin(theta)
    return table.reshape(4 * DEPTH, 2 * DEPTH)


def window_table():
    freq = np.arange(DEPTH)
    table = np.zeros((OFFS, 6, 16, DEPTH))
    low, high = (freq >= 1) & (freq < 64), freq > 64
    for index in range(OFFS):
        steps = np.arange(WIN) - REACH + index - MAX_OFF
        theta = angles(steps, freq, DEPTH)
        cos, sin = np.cos(theta), np.sin(theta)
        edge = 0.5 * cos * ((freq == 0) | (freq == 64))
        table[index, 0, :WIN] = cos
        table[index, 1, :WIN] = sin
        table[index, 2, :WIN] = cos * low + edge
        table[index, 3, :WIN] = sin * low
        table[index, 4, :WIN] = cos * high
        table[index, 5, :WIN] = edge - sin * high
    return table.reshape(OFFS, 96, DEPTH)


def plane_table():
    table = np.zeros((SUBS, 2, 2, HALF, 128))
    step = np.arange(WIN) - REACH
    ones = np.ones(WIN)
    for sub in range(SUBS):
        for half in range(2):
            freq = np.arange(HALF) + half
            theta_x = angles(freq, step, ALONG)
            theta_y = angles([across_freq(half, sub)], step, ACROSS)[0]
            theta = theta_y[None, :, None] + theta_x[:, None, :]
            table[sub, half, 0, :, : WIN * WIN] = np.cos(theta).reshape(HALF, -1)
            table[sub, half, 1, :, : WIN * WIN] = -np.sin(theta).reshape(HALF, -1)
    sign = np.where(step % 2 == 0, 1.0, -1.0)
    table[0, 0, 1, 0, : WIN * WIN] = np.outer(ones, sign).reshape(-1)
    table[0, 1, 1, HALF - 1, : WIN * WIN] = np.outer(sign, ones).reshape(-1)
    return table.reshape(SUBS, 4 * HALF, 128) * (2.0 / VOXELS)


def shift_table():
    table = np.zeros((2, 2, 16, HALF))
    for half in range(2):
        theta = angles(np.arange(OFFS) - MAX_OFF, np.arange(HALF) + half, ALONG)
        table[half, 0, :OFFS] = np.cos(theta)
        table[half, 1, :OFFS] = np.sin(theta)
    return table.reshape(4, 16, HALF).astype(np.float32)


def circle_table():
    theta = np.arange(ACROSS) * (2.0 * np.pi / ACROSS)
    return np.stack([np.cos(theta), np.sin(theta)]).astype(np.float32)


def graph_table():
    table = np.zeros((PLANES, 8, ROW * PLANES), np.float32)
    for plane in range(PLANES):
        base = ROW * plane
        pairs = [(base, base + 1), (base + 2, base + 3), (base + 1, base + 2)]
        pairs += [(base - ROW + col, base + col) for col in range(ROW)]
        for slot, (first, second) in enumerate(pairs):
            if first >= 0:
                table[plane, slot, first] = 1.0
                table[plane, slot, second] = -1.0
    return table.reshape(PLANES * 8, ROW * PLANES)


def dot(left, right):
    return jnp.dot(left, right, preferred_element_type=F32)


def split(value):
    high = value.astype(BF)
    return high, (value - high.astype(F32)).astype(BF)


def across_dft(strip, half, across_hi, across_lo):
    both = dot(across_hi[half], strip) + dot(across_lo[half], strip)
    rows = SUBS * LOCAL
    return jnp.concatenate([both[:rows], both[rows:]], axis=1)


def along_dft(value, half, along_hi, along_lo, extra, count):
    high, low = split(value)
    out = dot(high, along_hi[half]) + dot(low, along_hi[half]) + dot(high, along_lo[half])
    rows = SUBS * LOCAL
    edge_hi = jnp.concatenate([high[rows * k : rows * k + 16, :ALONG] for k in range(count)], axis=0)
    edge_lo = jnp.concatenate([low[rows * k : rows * k + 16, :ALONG] for k in range(count)], axis=0)
    more = dot(edge_hi, extra[half]) + dot(edge_lo, extra[half])
    pieces = []
    for k in range(count):
        block = out[rows * k : rows * (k + 1)]
        head = block[:LOCAL]
        head = jnp.concatenate(
            [head[:, :HALF], head[:, HALF:] + more[16 * k : 16 * k + LOCAL]], axis=1
        )
        pieces.append(jnp.concatenate([head, block[LOCAL:]], axis=0).reshape(SUBS, LOCAL, 2 * HALF))
    return pieces


def local_kernel(strips, ahi, alo, bhi, blo, extra, out):
    chosen = (1, 4, 2, 6)
    parts = []
    for half in range(2):
        stack = [across_dft(strips[k], half, ahi, alo) for k in chosen]
        parts.append(along_dft(jnp.concatenate(stack, axis=0), half, bhi, blo, extra, 4))
    for k in range(4):
        out[:, 16 * k : 16 * k + 16, :] = jnp.concatenate(
            [parts[0][k], parts[1][k]], axis=1
        ).astype(BF)


def remote_kernel(core, below, own, other, ahi, alo, bhi, blo, extra, ignored, out):
    del ignored
    parts = []
    for half in range(2):
        stack = [across_dft(below[k], half, ahi, alo) for k in range(2)]
        parts.append(along_dft(jnp.concatenate(stack, axis=0), half, bhi, blo, extra, 2))
    for k in range(2):
        out[:, 16 * k : 16 * k + 16, :] = jnp.concatenate(
            [parts[0][k], parts[1][k]], axis=1
        ).astype(BF)
    me = core[0]
    is_left = me == 0
    mine, theirs = own[...], other[...]
    first = jnp.where(is_left, mine, theirs)
    second = jnp.where(is_left, theirs, mine)
    stack = [across_dft(strip, me, ahi, alo) for strip in (first, second)]
    seam = along_dft(jnp.concatenate(stack, axis=0), me, bhi, blo, extra, 2)
    out[:, 32:48, :] = jnp.concatenate(seam, axis=1).astype(BF)


def spectrum_of(block, lanes, mhi, mlo):
    both = dot(mhi, block) + dot(mlo, block)
    cos, sin = both[: 2 * DEPTH], both[2 * DEPTH :]
    cos_re, cos_im = cos[:, :HALF], cos[:, HALF:]
    sin_re, sin_im = sin[:, :HALF], sin[:, HALF:]
    low, high = lanes
    real = jnp.where(low, cos_re, jnp.where(high, cos_im, cos_re + sin_im))
    imag = jnp.where(low, -sin_re, jnp.where(high, -sin_im, cos_im - sin_re))
    return real, imag


def phase_of(first, second, edge):
    floor = (FLOOR_SHARE * VOXELS) ** 2
    first_re, first_im = first
    second_re, second_im = second
    straight, crossed = first_re * second_re, first_im * second_im
    real = straight + jnp.where(edge, 0.0, crossed)
    imag = jnp.where(edge, crossed, first_im * second_re - first_re * second_im)
    real_sq, imag_sq = real * real, imag * imag
    norm = lax.rsqrt(real_sq + jnp.where(edge, 0.0, imag_sq) + floor)
    norm_im = jnp.where(edge, lax.rsqrt(imag_sq + floor), norm)
    return real * norm, imag * norm_im


def window_kernel(meta, circle, sub, core, got, mhi, mlo, vhi, vlo, ehi, elo, shift, out):
    d, c = sub[0], core[0]
    row = lax.broadcasted_iota(jnp.int32, (2 * DEPTH, HALF), 0)
    lane = lax.broadcasted_iota(jnp.int32, (2 * DEPTH, HALF), 1)
    freq = lax.rem(row, DEPTH)
    nowhere = jnp.where(d == 0, 0, 2 * HALF)

    def special(half_of_row):
        held = lane == half_of_row * (HALF - 1) + nowhere
        low = held & (freq > 0) & (freq < 64)
        high = held & (freq > 64)
        edge = held & ((freq == 0) | (freq == 64))
        return (low, high), edge

    lanes, edge = special(row // DEPTH)
    mh, ml = mhi[...], mlo[...]

    def spectrum(slot, masks):
        block = got[:, 16 * slot : 16 * slot + 16, :].reshape(2 * DEPTH, 2 * HALF)
        return spectrum_of(block, masks, mh, ml)

    small_lane = lax.broadcasted_iota(jnp.int32, (16, HALF), 1)

    def window_rows(phase, half, slot):
        off_z, off_y, off_x = meta[slot, 0], meta[slot, 1], meta[slot, 2]
        both = jnp.concatenate(phase, axis=1)
        high, low = split(both)
        table_hi, table_lo = vhi[off_z + MAX_OFF], vlo[off_z + MAX_OFF]
        rows = dot(table_hi, high) + dot(table_lo, high) + dot(table_hi, low)
        part = [(rows[16 * k : 16 * k + 16, :HALF], rows[16 * k : 16 * k + 16, HALF:]) for k in range(6)]
        real = part[0][0] - part[1][1]
        imag = part[1][0] + part[0][1]
        held = small_lane == half * (HALF - 1) + nowhere
        sign = jnp.where(lax.rem(off_x + 6, 2) == 0, 1.0, -1.0).astype(F32)
        real = jnp.where(held, part[2][0] - part[3][1], real)
        imag = jnp.where(held, (part[4][0] + part[5][1]) * sign, imag)
        freq_y = jnp.where(half == 0, d, jnp.where(d == 0, ACROSS // 2, ACROSS - d))
        turn = lax.rem(freq_y * (off_y + ACROSS), ACROSS)
        cos_y, sin_y = circle[0, turn], circle[1, turn]
        cos_x = shift[2 * half, pl.ds(off_x + MAX_OFF, 1), :]
        sin_x = shift[2 * half + 1, pl.ds(off_x + MAX_OFF, 1), :]
        cos = cos_x * cos_y - sin_x * sin_y
        sin = sin_x * cos_y + cos_x * sin_y
        return jnp.concatenate([real * cos - imag * sin, real * sin + imag * cos], axis=1)

    pieces = []
    for first, second, slot in ((0, 1, c), (4, 2, 3 + 2 * c), (5, 3, 4 + 2 * c)):
        real, imag = phase_of(spectrum(first, lanes), spectrum(second, lanes), edge)
        halves = [
            window_rows((real[DEPTH * h : DEPTH * (h + 1)], imag[DEPTH * h : DEPTH * (h + 1)]), h, slot)
            for h in range(2)
        ]
        pieces.append(jnp.concatenate(halves, axis=1))
    seam_lanes, seam_edge = special(c)
    real, imag = spectrum(6, seam_lanes)
    phase = phase_of(
        (real[:DEPTH], imag[:DEPTH]), (real[DEPTH:], imag[DEPTH:]), seam_edge[:DEPTH]
    )
    seam = window_rows(phase, c, 2)
    empty = jnp.zeros_like(seam)
    pieces.append(
        jnp.concatenate([jnp.where(c == 0, seam, empty), jnp.where(c == 0, empty, seam)], axis=1)
    )
    terms = jnp.concatenate(pieces, axis=0)
    high, low = split(terms)
    table_hi, table_lo = ehi[0], elo[0]
    sums = dot(high, table_hi) + dot(low, table_hi) + dot(high, table_lo)
    packed = jnp.concatenate(
        [sums[16 * k : 16 * k + WIN] for k in range(4)] + [jnp.zeros((4, 128), F32)], axis=0
    )
    out[...] = jnp.broadcast_to(packed[None], out.shape)


def energy_kernel(core, got, offsets, windows, terms):
    left = got[0]
    right = got[SUBS]
    for k in range(1, SUBS):
        left = left + got[k]
        right = right + got[SUBS + k]
    blocks = [left[:WIN], right[:WIN], left[27:36] + right[27:36]]
    blocks += [left[9:18], left[18:27], right[9:18], right[18:27]]
    step_z = (lax.broadcasted_iota(jnp.int32, (WIN, 128), 0) - REACH).astype(F32)
    sums, sums_z = [], []
    for block in blocks:
        square = block * block
        sums.append(jnp.sum(square, axis=0, keepdims=True))
        sums_z.append(jnp.sum(square * step_z, axis=0, keepdims=True))
    zero = jnp.zeros((1, 128), F32)
    sums = jnp.concatenate(sums + [zero], axis=0)
    sums_z = jnp.concatenate(sums_z + [zero], axis=0)
    lane = lax.broadcasted_iota(jnp.int32, (8, 128), 1)
    step_y = (lane // WIN - REACH).astype(F32)
    step_x = (lane % WIN - REACH).astype(F32)
    energy = jnp.sum(sums, axis=1, keepdims=True)
    moments = [sums_z, sums * step_y, sums * step_x]
    moments = [jnp.sum(m, axis=1, keepdims=True) for m in moments]
    mixed = jnp.where(lane == 1, moments[0], jnp.where(lane == 2, moments[1], moments[2]))
    place = offsets[...] + mixed / (energy + EPSILON)
    value = jnp.where(lane == 0, energy, energy * place)
    value = jnp.where(lane < 4, value, 0.0)
    terms[...] = jnp.broadcast_to(value[None], terms.shape)
    is_left = core[0] == 0
    mine = [
        jnp.where(is_left, blocks[0], blocks[1]),
        blocks[2],
        jnp.where(is_left, blocks[3], blocks[5]),
        jnp.where(is_left, blocks[4], blocks[6]),
    ]
    for k in range(4):
        windows[k, :WIN, :] = mine[k]
        windows[k, WIN:, :] = jnp.zeros((16 - WIN, 128), F32)


def final_kernel(meta, mine, below, terms, graph, windows, matrix, rhs):
    slot = lax.broadcasted_iota(jnp.int32, (6, 128), 0)
    blocks = [mine[k] for k in range(4)] + [below[k] for k in range(2)]
    places = [slot == meta[9 + k, 0] for k in range(6)]
    for step in range(WIN):
        rows = jnp.zeros((6, 128), F32)
        for block, place in zip(blocks, places):
            rows = jnp.where(place, block[step : step + 1], rows)
        windows[:, WIN * WIN * step : WIN * WIN * (step + 1)] = rows[:, : WIN * WIN]
    table = graph[...]
    value = terms[...].reshape(PLANES * 8, 128)
    weighted = table * value[:, :1]
    over = (((0,), (0,)), ((), ()))
    matrix[...] = lax.dot_general(
        table, weighted, over, precision=lax.Precision.HIGHEST, preferred_element_type=F32
    )
    load = lax.dot_general(
        table, value, over, precision=lax.Precision.HIGHEST, preferred_element_type=F32
    )
    rhs[...] = load[:, 1:4]


def pair_facts(pair_tiles, pair_owner, pair_offset, plane, core):
    count = pair_owner.shape[0]
    key = pair_tiles[:, 0] * 2 + (pair_tiles[:, 1] - pair_tiles[:, 0] != 1)
    base = ROW * plane
    here = [base, base + 2, base + 1]
    up = [base - ROW + col for col in range(ROW)]
    down = [base + 2 * core, base + 2 * core + 1]
    wanted = jnp.stack([2 * t for t in here] + [2 * t + 1 for t in up + down])
    match = (wanted[:, None] == key[None, :]).astype(jnp.int32)
    owned = (pair_owner == 2 * plane + core).astype(jnp.int32)
    place = jnp.arange(count, dtype=jnp.int32)
    offset = jnp.sum(match[:, :, None] * pair_offset[None], axis=1)
    at = jnp.sum(match * place[None], axis=1)
    held = jnp.sum(match * owned[None], axis=1)
    ordinal = jnp.sum((place[None] < at[:, None]).astype(jnp.int32) * owned[None], axis=1)
    row = jnp.where(held > 0, ordinal, -1)
    mine = jnp.stack(
        [
            jnp.where(core == 0, row[0], row[1]),
            row[2],
            jnp.where(core == 0, row[3], row[5]),
            jnp.where(core == 0, row[4], row[6]),
            row[7],
            row[8],
        ]
    )
    facts = jnp.concatenate([offset, jnp.broadcast_to(mine[:, None], (6, 3))], axis=0)
    lanes = jnp.zeros((8, 128), F32).at[:7, 1:4].set(offset[:7].astype(F32))
    return facts, lanes


def call(kernel, shapes, operands, spaces, aliases=None, **params):
    specs = [pl.BlockSpec(memory_space=space) for space in spaces]
    outs = jax.tree.map(lambda _: pl.BlockSpec(memory_space=pltpu.VMEM), shapes)
    return pl.pallas_call(
        kernel,
        out_shape=shapes,
        in_specs=specs,
        out_specs=outs,
        compiler_params=pltpu.CompilerParams(vmem_limit_bytes=40 * 1024 * 1024),
        **params,
    )(*operands)


def local(strips, pair_tiles, pair_owner, pair_offset):
    plane, core, sub = (lax.axis_index(name) for name in ("z", "core", "sub"))
    ahi, alo = split_np(across_table())
    bhi, blo = split_np(along_table())
    extra = extra_table().astype(ml_dtypes.bfloat16)
    mhi, mlo = split_np(depth_table())
    vhi, vlo = split_np(window_table())
    ehi, elo = split_np(plane_table())
    vmem, smem = pltpu.VMEM, pltpu.SMEM
    core_arr = core.reshape(1).astype(jnp.int32)
    sub_arr = sub.reshape(1).astype(jnp.int32)

    tiles = strips.reshape(8, LOCAL * ACROSS, ALONG)
    from_above = lax.ppermute(
        jnp.stack([tiles[3], tiles[7]]), "z", [(k, k + 1) for k in range(PLANES - 1)]
    )
    own = jnp.where(core == 0, tiles[5], tiles[0])
    other = lax.ppermute(own, "core", [(0, 1), (1, 0)])
    facts, lanes = pair_facts(pair_tiles, pair_owner, pair_offset, plane, core)

    tables = (ahi, alo, bhi, blo, extra)
    here = call(
        local_kernel,
        jax.ShapeDtypeStruct((SUBS, 64, 2 * HALF), BF),
        (tiles,) + tables,
        (vmem,) * 6,
    )
    there = call(
        remote_kernel,
        jax.ShapeDtypeStruct((SUBS, 48, 2 * HALF), BF),
        (core_arr, from_above, own, other) + tables + (core_arr,),
        (smem,) + (vmem,) * 8 + (smem,),
    )
    sent = jnp.concatenate([here, there], axis=1)
    got = lax.all_to_all(sent, "sub", split_axis=0, concat_axis=0, tiled=True)

    ehi_here = lax.dynamic_slice_in_dim(jnp.asarray(ehi), sub, 1, 0)
    elo_here = lax.dynamic_slice_in_dim(jnp.asarray(elo), sub, 1, 0)
    partial = call(
        window_kernel,
        jax.ShapeDtypeStruct((2 * SUBS, 40, 128), F32),
        (facts, circle_table(), sub_arr, core_arr, got, mhi, mlo, vhi, vlo, ehi_here, elo_here, shift_table()),
        (smem,) * 4 + (vmem,) * 8,
    )
    shares = lax.all_to_all(partial, ("core", "sub"), split_axis=0, concat_axis=0, tiled=True)
    mine, terms = call(
        energy_kernel,
        (jax.ShapeDtypeStruct((4, 16, 128), F32), jax.ShapeDtypeStruct((PLANES, 8, 128), F32)),
        (core_arr, shares, lanes),
        (smem, vmem, vmem),
    )
    below = lax.ppermute(mine[2:], "z", [(k + 1, k) for k in range(PLANES - 1)])
    all_terms = lax.all_to_all(terms, "z", split_axis=0, concat_axis=0, tiled=True)
    return call(
        final_kernel,
        (
            jax.ShapeDtypeStruct((6, WIN * WIN * WIN), F32),
            jax.ShapeDtypeStruct((64, 64), F32),
            jax.ShapeDtypeStruct((64, 3), F32),
        ),
        (facts, mine, below, all_terms, graph_table()),
        (smem,) + (vmem,) * 4,
    )


def solution(mesh):
    grid = Mesh(mesh.devices.reshape(PLANES, 2, SUBS), ("z", "core", "sub"))
    tiles = ("z", "core")
    in_specs = (P(tiles, None, "sub", None, None), P(), P(), P())
    out_specs = (P(tiles, None), P(), P())
    return jax.shard_map(local, mesh=grid, in_specs=in_specs, out_specs=out_specs, check_vma=False)
```

```python
import jax
import jax.numpy as jnp
import ml_dtypes
import numpy as np
from jax import lax
from jax.experimental import pallas as pl
from jax.experimental.pallas import tpu as pltpu
from jax.sharding import Mesh, PartitionSpec as P

REACH = 4
WIN = 9
EPSILON = 1e-06
FLOOR_SHARE = 0.05
ROW = 4
PLANES = 16
SUBS = 16
DEPTH, ACROSS, ALONG = 128, 32, 256
LOCAL = DEPTH // SUBS
HALF = ALONG // 2
VOXELS = DEPTH * ACROSS * ALONG
MAX_OFF = 5
OFFS = 2 * MAX_OFF + 1
SLOTS = 7
BF = jnp.bfloat16
F32 = jnp.float32


def split_np(table):
    high = table.astype(ml_dtypes.bfloat16)
    low = (table - high.astype(np.float64)).astype(ml_dtypes.bfloat16)
    return high, low


def lane_tiles(table):
    return np.stack([table[..., :128], table[..., 128:]], axis=-3)


def angles(rows, cols, length):
    return (np.outer(rows, cols) % length) * (2.0 * np.pi / length)


def across_freq(half, sub):
    if half == 0:
        return sub
    return ACROSS // 2 if sub == 0 else ACROSS - sub


def across_table():
    table = np.zeros((2, 2, SUBS, LOCAL, LOCAL, ACROSS))
    for half in range(2):
        for sub in range(SUBS):
            theta = angles([across_freq(half, sub)], np.arange(ACROSS), ACROSS)[0]
            for plane in range(LOCAL):
                table[half, 0, sub, plane, plane] = np.cos(theta)
                table[half, 1, sub, plane, plane] = -np.sin(theta)
    return table.reshape(2, 2 * SUBS * LOCAL, LOCAL * ACROSS)


def along_table():
    table = np.zeros((2, 2, ALONG, 2, HALF))
    for half in range(2):
        theta = angles(np.arange(ALONG), np.arange(HALF) + half, ALONG)
        table[half, 0, :, 0] = np.cos(theta)
        table[half, 0, :, 1] = -np.sin(theta)
        table[half, 1, :, 0] = np.sin(theta)
        table[half, 1, :, 1] = np.cos(theta)
    return table.reshape(2, 2 * ALONG, 2 * HALF)


def extra_table():
    table = np.zeros((2, ALONG, HALF))
    table[0, :, 0] = np.where(np.arange(ALONG) % 2 == 0, 1.0, -1.0)
    table[1, :, HALF - 1] = 1.0
    return table


HALF_ROWS = 2 * SUBS * LOCAL


def plane_dft_tables():
    across, along = split_np(across_table()), split_np(along_table())
    extra = extra_table().astype(ml_dtypes.bfloat16)
    pieces = [part[half] for half in range(2) for part in across]
    pieces += [part[half] for half in range(2) for part in along]
    pieces.append(np.concatenate([extra[0], extra[1]], axis=1))
    return lane_tiles(np.concatenate(pieces, axis=0))


def wide_rows(tables, start, count):
    rows = pl.ds(pl.multiple_of(start, 256), count)
    return jnp.concatenate([tables[0, rows, :], tables[1, rows, :]], axis=1)


def across_rows(tables, half, low):
    return wide_rows(tables, (2 * half + low) * HALF_ROWS, HALF_ROWS)


def along_rows(tables, half, low):
    start = 4 * HALF_ROWS + (2 * half + low) * 2 * ALONG
    return wide_rows(tables, start, 2 * ALONG)


def extra_rows(tables, half):
    start = 4 * HALF_ROWS + 8 * ALONG
    return tables[half, start : start + ALONG, :]


def depth_table():
    theta = angles(np.arange(DEPTH), np.arange(DEPTH), DEPTH).reshape(DEPTH, SUBS, LOCAL)
    table = np.zeros((2, 2, DEPTH, SUBS, 2, LOCAL))
    for half in range(2):
        table[0, half, :, :, half, :] = np.cos(theta)
        table[1, half, :, :, half, :] = np.sin(theta)
    return table.reshape(4 * DEPTH, 2 * DEPTH)


def window_table():
    freq = np.arange(DEPTH)
    table = np.zeros((OFFS, 6, 16, DEPTH))
    low, high = (freq >= 1) & (freq < 64), freq > 64
    for index in range(OFFS):
        steps = np.arange(WIN) - REACH + index - MAX_OFF
        theta = angles(steps, freq, DEPTH)
        cos, sin = np.cos(theta), np.sin(theta)
        edge = 0.5 * cos * ((freq == 0) | (freq == 64))
        table[index, 0, :WIN] = cos
        table[index, 1, :WIN] = sin
        table[index, 2, :WIN] = cos * low + edge
        table[index, 3, :WIN] = sin * low
        table[index, 4, :WIN] = cos * high
        table[index, 5, :WIN] = edge - sin * high
    return table.reshape(OFFS, 96, DEPTH)


def plane_table():
    table = np.zeros((SUBS, 2, 2, HALF, 128))
    step = np.arange(WIN) - REACH
    ones = np.ones(WIN)
    for sub in range(SUBS):
        for half in range(2):
            freq = np.arange(HALF) + half
            theta_x = angles(freq, step, ALONG)
            theta_y = angles([across_freq(half, sub)], step, ACROSS)[0]
            theta = theta_y[None, :, None] + theta_x[:, None, :]
            table[sub, half, 0, :, : WIN * WIN] = np.cos(theta).reshape(HALF, -1)
            table[sub, half, 1, :, : WIN * WIN] = -np.sin(theta).reshape(HALF, -1)
    sign = np.where(step % 2 == 0, 1.0, -1.0)
    table[0, 0, 1, 0, : WIN * WIN] = np.outer(ones, sign).reshape(-1)
    table[0, 1, 1, HALF - 1, : WIN * WIN] = np.outer(sign, ones).reshape(-1)
    return table.reshape(SUBS, 4 * HALF, 128) * (2.0 / VOXELS)


def shift_table():
    table = np.zeros((2, 2, 16, HALF))
    for half in range(2):
        theta = angles(np.arange(OFFS) - MAX_OFF, np.arange(HALF) + half, ALONG)
        table[half, 0, :OFFS] = np.cos(theta)
        table[half, 1, :OFFS] = np.sin(theta)
    return table.reshape(4, 16, HALF).astype(np.float32)


def circle_table():
    theta = np.arange(ACROSS) * (2.0 * np.pi / ACROSS)
    return np.stack([np.cos(theta), np.sin(theta)]).astype(np.float32)


def graph_table():
    table = np.zeros((PLANES, 8, ROW * PLANES), np.float32)
    for plane in range(PLANES):
        base = ROW * plane
        pairs = [(base, base + 1), (base + 2, base + 3), (base + 1, base + 2)]
        pairs += [(base - ROW + col, base + col) for col in range(ROW)]
        for slot, (first, second) in enumerate(pairs):
            if first >= 0:
                table[plane, slot, first] = 1.0
                table[plane, slot, second] = -1.0
    return table.reshape(PLANES * 8, ROW * PLANES)


def dot(left, right):
    return jnp.dot(left, right, preferred_element_type=F32)


def split(value):
    high = value.astype(BF)
    return high, (value - high.astype(F32)).astype(BF)


def across_dft(strip, half, tables):
    both = dot(across_rows(tables, half, 0), strip) + dot(across_rows(tables, half, 1), strip)
    rows = SUBS * LOCAL
    return jnp.concatenate([both[:rows], both[rows:]], axis=1)


def along_dft(value, half, tables, count):
    high, low = split(value)
    table_hi, table_lo = along_rows(tables, half, 0), along_rows(tables, half, 1)
    out = dot(high, table_hi) + dot(low, table_hi) + dot(high, table_lo)
    extra = extra_rows(tables, half)
    rows = SUBS * LOCAL
    edge_hi = jnp.concatenate([high[rows * k : rows * k + 16, :ALONG] for k in range(count)], axis=0)
    edge_lo = jnp.concatenate([low[rows * k : rows * k + 16, :ALONG] for k in range(count)], axis=0)
    more = dot(edge_hi, extra) + dot(edge_lo, extra)
    pieces = []
    for k in range(count):
        block = out[rows * k : rows * (k + 1)]
        head = block[:LOCAL]
        head = jnp.concatenate(
            [head[:, :HALF], head[:, HALF:] + more[16 * k : 16 * k + LOCAL]], axis=1
        )
        pieces.append(jnp.concatenate([head, block[LOCAL:]], axis=0).reshape(SUBS, LOCAL, 2 * HALF))
    return pieces


def pair_facts(where, pair_tiles, owner, pair_offset):
    plane, core = where[0], where[1]
    base = ROW * plane
    count = owner.shape[1]
    row = lax.broadcasted_iota(jnp.int32, (16, count), 0)
    place = lax.broadcasted_iota(jnp.int32, (16, count), 1)
    home = 2 * base + jnp.where(row == 1, 4, jnp.where(row == 2, 2, 0))
    up = 2 * (base - ROW + row - 3) + 1
    down = 2 * (base + 2 * core + row - 7) + 1
    wanted = jnp.where(row < 3, home, jnp.where(row < 7, up, jnp.where(row < 9, down, -100)))
    first, second = pair_tiles[0:1, :], pair_tiles[1:2, :]
    key = first * 2 + jnp.where(second - first == 1, 0, 1)
    match = wanted == key
    owned = jnp.broadcast_to(owner[...] == 2 * plane + core, match.shape)

    def total(mask, value):
        return jnp.sum(jnp.where(mask, value, 0), axis=1, keepdims=True)

    offset = [total(match, jnp.broadcast_to(pair_offset[k : k + 1, :], match.shape)) for k in range(3)]
    at = total(match, place)
    held = total(match & owned, 1)
    ordinal = total((place < at) & owned, 1)
    return offset, jnp.where(held > 0, ordinal, -1)


def facts_kernel(where, pair_tiles, owner, pair_offset, ignored, facts, offsets):
    del ignored
    offset, slot = pair_facts(where, pair_tiles, owner, pair_offset)
    lane = lax.broadcasted_iota(jnp.int32, (16, 128), 1)
    facts[...] = jnp.where(
        lane == 0, offset[0], jnp.where(lane == 1, offset[1], jnp.where(lane == 2, offset[2], slot))
    )
    lane = lane[:8]
    offsets[...] = jnp.where(
        lane == 1, offset[0][:8], jnp.where(lane == 2, offset[1][:8], offset[2][:8])
    ).astype(F32)


def local_kernel(strips, tables, out):
    chosen = (1, 4, 2, 6)
    parts = []
    for half in range(2):
        stack = [across_dft(strips[k], half, tables) for k in chosen]
        parts.append(along_dft(jnp.concatenate(stack, axis=0), half, tables, 4))
    for k in range(4):
        out[:, 16 * k : 16 * k + 16, :] = jnp.concatenate(
            [parts[0][k], parts[1][k]], axis=1
        ).astype(BF)


def remote_kernel(where, here, below, own, other, tables, ignored, out):
    del here, ignored
    parts = []
    for half in range(2):
        stack = [across_dft(below[k], half, tables) for k in range(2)]
        parts.append(along_dft(jnp.concatenate(stack, axis=0), half, tables, 2))
    for k in range(2):
        out[:, 64 + 16 * k : 80 + 16 * k, :] = jnp.concatenate(
            [parts[0][k], parts[1][k]], axis=1
        ).astype(BF)
    core = where[1]
    mine, theirs = own[...], other[...]
    first = jnp.where(core == 0, mine, theirs)
    second = jnp.where(core == 0, theirs, mine)
    stack = [across_dft(strip, core, tables) for strip in (first, second)]
    seam = along_dft(jnp.concatenate(stack, axis=0), core, tables, 2)
    out[:, 96:112, :] = jnp.concatenate(seam, axis=1).astype(BF)


def spectrum_of(block, lanes, mhi, mlo):
    both = dot(mhi, block) + dot(mlo, block)
    cos, sin = both[: 2 * DEPTH], both[2 * DEPTH :]
    cos_re, cos_im = cos[:, :HALF], cos[:, HALF:]
    sin_re, sin_im = sin[:, :HALF], sin[:, HALF:]
    low, high = lanes
    real = jnp.where(low, cos_re, jnp.where(high, cos_im, cos_re + sin_im))
    imag = jnp.where(low, -sin_re, jnp.where(high, -sin_im, cos_im - sin_re))
    return real, imag


def phase_of(first, second, edge):
    floor = (FLOOR_SHARE * VOXELS) ** 2
    first_re, first_im = first
    second_re, second_im = second
    straight, crossed = first_re * second_re, first_im * second_im
    real = straight + jnp.where(edge, 0.0, crossed)
    imag = jnp.where(edge, crossed, first_im * second_re - first_re * second_im)
    real_sq, imag_sq = real * real, imag * imag
    norm = lax.rsqrt(real_sq + jnp.where(edge, 0.0, imag_sq) + floor)
    norm_im = jnp.where(edge, lax.rsqrt(imag_sq + floor), norm)
    return real * norm, imag * norm_im


def window_kernel(where, meta, circle, got, depth, vhi, vlo, planes, shift, out, table, arrived):
    c, d = where[1], where[2]
    fetch = pltpu.make_async_copy(planes.at[d], table, arrived)
    fetch.start()
    row = lax.broadcasted_iota(jnp.int32, (2 * DEPTH, HALF), 0)
    lane = lax.broadcasted_iota(jnp.int32, (2 * DEPTH, HALF), 1)
    freq = lax.rem(row, DEPTH)
    nowhere = jnp.where(d == 0, 0, 2 * HALF)

    def special(half_of_row):
        held = lane == half_of_row * (HALF - 1) + nowhere
        low = held & (freq > 0) & (freq < 64)
        high = held & (freq > 64)
        edge = held & ((freq == 0) | (freq == 64))
        return (low, high), edge

    lanes, edge = special(row // DEPTH)
    mh, ml = wide_rows(depth, 0, 512), wide_rows(depth, 512, 512)

    def spectrum(slot, masks):
        block = got[:, 16 * slot : 16 * slot + 16, :].reshape(2 * DEPTH, 2 * HALF)
        return spectrum_of(block, masks, mh, ml)

    small_lane = lax.broadcasted_iota(jnp.int32, (16, HALF), 1)

    def window_rows(phase, half, slot):
        off_z, off_y, off_x = meta[slot, 0], meta[slot, 1], meta[slot, 2]
        both = jnp.concatenate(phase, axis=1)
        high, low = split(both)
        table_hi, table_lo = vhi[off_z + MAX_OFF], vlo[off_z + MAX_OFF]
        rows = dot(table_hi, high) + dot(table_lo, high) + dot(table_hi, low)
        part = [(rows[16 * k : 16 * k + 16, :HALF], rows[16 * k : 16 * k + 16, HALF:]) for k in range(6)]
        real = part[0][0] - part[1][1]
        imag = part[1][0] + part[0][1]
        held = small_lane == half * (HALF - 1) + nowhere
        sign = jnp.where(lax.rem(off_x + 6, 2) == 0, 1.0, -1.0).astype(F32)
        real = jnp.where(held, part[2][0] - part[3][1], real)
        imag = jnp.where(held, (part[4][0] + part[5][1]) * sign, imag)
        freq_y = jnp.where(half == 0, d, jnp.where(d == 0, ACROSS // 2, ACROSS - d))
        turn = lax.rem(freq_y * (off_y + ACROSS), ACROSS)
        cos_y, sin_y = circle[0, turn], circle[1, turn]
        cos_x = shift[2 * half, pl.ds(off_x + MAX_OFF, 1), :]
        sin_x = shift[2 * half + 1, pl.ds(off_x + MAX_OFF, 1), :]
        cos = cos_x * cos_y - sin_x * sin_y
        sin = sin_x * cos_y + cos_x * sin_y
        return jnp.concatenate([real * cos - imag * sin, real * sin + imag * cos], axis=1)

    pieces = []
    for first, second, slot in ((0, 1, c), (4, 2, 3 + 2 * c), (5, 3, 4 + 2 * c)):
        real, imag = phase_of(spectrum(first, lanes), spectrum(second, lanes), edge)
        halves = [
            window_rows((real[DEPTH * h : DEPTH * (h + 1)], imag[DEPTH * h : DEPTH * (h + 1)]), h, slot)
            for h in range(2)
        ]
        pieces.append(jnp.concatenate(halves, axis=1))
    seam_lanes, seam_edge = special(c)
    real, imag = spectrum(6, seam_lanes)
    phase = phase_of(
        (real[:DEPTH], imag[:DEPTH]), (real[DEPTH:], imag[DEPTH:]), seam_edge[:DEPTH]
    )
    seam = window_rows(phase, c, 2)
    empty = jnp.zeros_like(seam)
    pieces.append(
        jnp.concatenate([jnp.where(c == 0, seam, empty), jnp.where(c == 0, empty, seam)], axis=1)
    )
    terms = jnp.concatenate(pieces, axis=0)
    high, low = split(terms)
    fetch.wait()
    both = jnp.concatenate([table[0], table[1]], axis=1)
    sums = dot(high, both) + jnp.concatenate(
        [dot(low, both[:, :128]), jnp.zeros((64, 128), F32)], axis=1
    )
    sums = sums[:, :128] + sums[:, 128:]
    wide = jnp.zeros((12, 256), F32)
    for third in range(3):
        rows = [sums[16 * k + 3 * third : 16 * k + 3 * third + 3] for k in range(4)]
        rows = jnp.concatenate([jnp.concatenate(rows, axis=0), jnp.zeros((12, 128), F32)], axis=1)
        wide = wide + (pltpu.roll(rows, 81 * third, 1) if third else rows)
    packed = jnp.concatenate([wide[:, :128], wide[:, 128:]], axis=0)
    out[...] = jnp.broadcast_to(packed[None], out.shape)


def unpack(packed):
    wide = jnp.concatenate([packed[:12], packed[12:]], axis=1)
    lane = lax.broadcasted_iota(jnp.int32, (12, 128), 1)
    thirds = []
    for third in range(3):
        rows = pltpu.roll(wide, 256 - 81 * third, 1) if third else wide
        thirds.append(jnp.where(lane < WIN * WIN, rows[:, :128], 0.0))
    return [jnp.concatenate([t[3 * k : 3 * k + 3] for t in thirds], axis=0) for k in range(4)]


def energy_kernel(where, got, offsets, windows, terms):
    left = got[0]
    right = got[SUBS]
    for k in range(1, SUBS):
        left = left + got[k]
        right = right + got[SUBS + k]
    left, right = unpack(left), unpack(right)
    blocks = [left[0], right[0], left[3] + right[3], left[1], left[2], right[1], right[2]]
    step_z = (lax.broadcasted_iota(jnp.int32, (WIN, 128), 0) - REACH).astype(F32)
    sums, sums_z = [], []
    for block in blocks:
        square = block * block
        sums.append(jnp.sum(square, axis=0, keepdims=True))
        sums_z.append(jnp.sum(square * step_z, axis=0, keepdims=True))
    zero = jnp.zeros((1, 128), F32)
    sums = jnp.concatenate(sums + [zero], axis=0)
    sums_z = jnp.concatenate(sums_z + [zero], axis=0)
    lane = lax.broadcasted_iota(jnp.int32, (8, 128), 1)
    step_y = (lane // WIN - REACH).astype(F32)
    step_x = (lane % WIN - REACH).astype(F32)
    energy = jnp.sum(sums, axis=1, keepdims=True)
    moments = [sums_z, sums * step_y, sums * step_x]
    moments = [jnp.sum(m, axis=1, keepdims=True) for m in moments]
    mixed = jnp.where(lane == 1, moments[0], jnp.where(lane == 2, moments[1], moments[2]))
    place = offsets[...] + mixed / (energy + EPSILON)
    value = jnp.where(lane == 0, energy, energy * place)
    value = jnp.where(lane < 4, value, 0.0)
    terms[...] = jnp.broadcast_to(value[None], terms.shape)
    is_left = where[1] == 0
    mine = [
        jnp.where(is_left, blocks[0], blocks[1]),
        blocks[2],
        jnp.where(is_left, blocks[3], blocks[5]),
        jnp.where(is_left, blocks[4], blocks[6]),
    ]
    for k in range(4):
        windows[k, :WIN, :] = mine[k]
        windows[k, WIN:, :] = jnp.zeros((16 - WIN, 128), F32)


def graph_kernel(terms, graph, ignored, matrix, rhs):
    del ignored
    table = graph[...]
    value = terms[...].reshape(PLANES * 8, 128)
    weighted = table * value[:, :1]
    over = (((0,), (0,)), ((), ()))
    matrix[...] = lax.dot_general(
        table, weighted, over, precision=lax.Precision.HIGHEST, preferred_element_type=F32
    )
    load = lax.dot_general(
        value, table, over, precision=lax.Precision.HIGHEST, preferred_element_type=F32
    )
    rhs[...] = load[1:4]


def place_kernel(where, meta, mine, below, windows, done):
    done[...] = mine[0, :8]
    c = where[1]
    slot = lax.broadcasted_iota(jnp.int32, (6, 128), 0)
    blocks = [mine[k] for k in range(4)] + [below[k] for k in range(2)]
    places = [slot == meta[k, 3] for k in (c, 2, 3 + 2 * c, 4 + 2 * c, 7, 8)]
    for step in range(WIN):
        rows = jnp.zeros((6, 128), F32)
        for block, place in zip(blocks, places):
            rows = jnp.where(place, block[step : step + 1], rows)
        windows[:, WIN * WIN * step : WIN * WIN * (step + 1)] = rows[:, : WIN * WIN]


def call(kernel, shapes, operands, spaces, **params):
    specs = [pl.BlockSpec(memory_space=space) for space in spaces]
    outs = jax.tree.map(lambda _: pl.BlockSpec(memory_space=pltpu.VMEM), shapes)
    return pl.pallas_call(
        kernel,
        out_shape=shapes,
        in_specs=specs,
        out_specs=outs,
        compiler_params=pltpu.CompilerParams(vmem_limit_bytes=40 * 1024 * 1024),
        **params,
    )(*operands)


def local(strips, pair_tiles, pair_owner, pair_offset):
    where = jnp.stack([lax.axis_index(name) for name in ("z", "core", "sub")]).astype(jnp.int32)
    core = where[1]
    tables = plane_dft_tables()
    depth = lane_tiles(np.concatenate(split_np(depth_table()), axis=0))
    vhi, vlo = split_np(window_table())
    planes = np.stack(split_np(plane_table()), axis=1)
    vmem, smem = pltpu.VMEM, pltpu.SMEM

    tiles = strips.reshape(8, LOCAL * ACROSS, ALONG)
    bottoms = jnp.stack([tiles[3], tiles[7]])
    from_above = lax.ppermute(bottoms, "z", [(k, k + 1) for k in range(PLANES - 1)])
    core_after, bottoms = lax.optimization_barrier((core, bottoms))
    own = lax.dynamic_index_in_dim(tiles, 5 - 5 * core_after, 0, keepdims=False)
    other = lax.ppermute(own, "core", [(0, 1), (1, 0)])

    chunks = jax.ShapeDtypeStruct((SUBS, 16 * SLOTS, 2 * HALF), BF)
    here = call(local_kernel, chunks, (tiles, tables), (vmem, vmem))
    facts, offsets = call(
        facts_kernel,
        (jax.ShapeDtypeStruct((16, 128), jnp.int32), jax.ShapeDtypeStruct((8, 128), F32)),
        (where, pair_tiles.T, pair_owner.reshape(1, -1), pair_offset.T, here),
        (smem,) + (vmem,) * 3 + (pl.ANY,),
    )
    sent = call(
        remote_kernel,
        chunks,
        (where, here, from_above, own, other, tables, offsets),
        (smem, vmem, vmem, vmem, vmem, vmem, pl.ANY),
        input_output_aliases={1: 0},
    )
    got = lax.all_to_all(sent, "sub", split_axis=0, concat_axis=0, tiled=True)
    partial = call(
        window_kernel,
        jax.ShapeDtypeStruct((2 * SUBS, 24, 128), F32),
        (where, facts, circle_table(), got, depth, vhi, vlo, planes, shift_table()),
        (smem,) * 3 + (vmem,) * 4 + (pltpu.HBM, vmem),
        scratch_shapes=[pltpu.VMEM((2, 4 * HALF, 128), BF), pltpu.SemaphoreType.DMA],
    )
    shares = lax.all_to_all(partial, ("core", "sub"), split_axis=0, concat_axis=0, tiled=True)
    mine, terms = call(
        energy_kernel,
        (jax.ShapeDtypeStruct((4, 16, 128), F32), jax.ShapeDtypeStruct((PLANES, 8, 128), F32)),
        (where, shares, offsets),
        (smem, vmem, vmem),
    )
    below = lax.ppermute(mine[2:], "z", [(k + 1, k) for k in range(PLANES - 1)])
    all_terms = lax.all_to_all(terms, "z", split_axis=0, concat_axis=0, tiled=True)
    windows, done = call(
        place_kernel,
        (jax.ShapeDtypeStruct((6, WIN * WIN * WIN), F32), jax.ShapeDtypeStruct((8, 128), F32)),
        (where, facts, mine, below),
        (smem, smem, vmem, vmem),
    )
    matrix, rhs = call(
        graph_kernel,
        (jax.ShapeDtypeStruct((64, 64), F32), jax.ShapeDtypeStruct((3, 64), F32)),
        (all_terms, graph_table(), done),
        (vmem, vmem, pl.ANY),
    )
    return windows, matrix, rhs.T


def solution(mesh):
    grid = Mesh(mesh.devices.reshape(PLANES, 2, SUBS), ("z", "core", "sub"))
    tiles = ("z", "core")
    in_specs = (P(tiles, None, "sub", None, None), P(), P(), P())
    out_specs = (P(tiles, None), P(), P())
    return jax.shard_map(local, mesh=grid, in_specs=in_specs, out_specs=out_specs, check_vma=False)
```

```python
import jax
import jax.numpy as jnp
import ml_dtypes
import numpy as np
from jax import lax
from jax.experimental import pallas as pl
from jax.experimental.pallas import tpu as pltpu
from jax.sharding import Mesh, PartitionSpec as P

REACH = 4
WIN = 9
EPSILON = 1e-06
FLOOR_SHARE = 0.05
ROW = 4
PLANES = 16
SUBS = 16
DEPTH, ACROSS, ALONG = 128, 32, 256
LOCAL = DEPTH // SUBS
HALF = ALONG // 2
VOXELS = DEPTH * ACROSS * ALONG
MAX_OFF = 5
OFFS = 2 * MAX_OFF + 1
BF = jnp.bfloat16
F32 = jnp.float32


def split_np(table):
    high = table.astype(ml_dtypes.bfloat16)
    low = (table - high.astype(np.float64)).astype(ml_dtypes.bfloat16)
    return high, low


def lane_tiles(table):
    return np.stack([table[..., :128], table[..., 128:]], axis=-3)


def angles(rows, cols, length):
    return (np.outer(rows, cols) % length) * (2.0 * np.pi / length)


def across_freq(half, sub):
    if half == 0:
        return sub
    return ACROSS // 2 if sub == 0 else ACROSS - sub


def across_table():
    table = np.zeros((2, 2, SUBS, LOCAL, LOCAL, ACROSS))
    for half in range(2):
        for sub in range(SUBS):
            theta = angles([across_freq(half, sub)], np.arange(ACROSS), ACROSS)[0]
            for plane in range(LOCAL):
                table[half, 0, sub, plane, plane] = np.cos(theta)
                table[half, 1, sub, plane, plane] = -np.sin(theta)
    return table.reshape(2, 2 * SUBS * LOCAL, LOCAL * ACROSS)


def along_table():
    table = np.zeros((2, 2, ALONG, 2, HALF))
    for half in range(2):
        theta = angles(np.arange(ALONG), np.arange(HALF) + half, ALONG)
        table[half, 0, :, 0] = np.cos(theta)
        table[half, 0, :, 1] = -np.sin(theta)
        table[half, 1, :, 0] = np.sin(theta)
        table[half, 1, :, 1] = np.cos(theta)
    return table.reshape(2, 2 * ALONG, 2 * HALF)


def extra_table():
    table = np.zeros((2, ALONG, HALF))
    table[0, :, 0] = np.where(np.arange(ALONG) % 2 == 0, 1.0, -1.0)
    table[1, :, HALF - 1] = 1.0
    return table


HALF_ROWS = 2 * SUBS * LOCAL


def plane_dft_tables():
    across, along = split_np(across_table()), split_np(along_table())
    extra = extra_table().astype(ml_dtypes.bfloat16)
    pieces = [part[half] for half in range(2) for part in across]
    pieces += [part[half] for half in range(2) for part in along]
    pieces.append(np.concatenate([extra[0], extra[1]], axis=1))
    return lane_tiles(np.concatenate(pieces, axis=0))


def wide_rows(tables, start, count):
    rows = pl.ds(pl.multiple_of(start, 256), count)
    return jnp.concatenate([tables[0, rows, :], tables[1, rows, :]], axis=1)


def across_rows(tables, half, low):
    return wide_rows(tables, (2 * half + low) * HALF_ROWS, HALF_ROWS)


def along_rows(tables, half, low):
    start = 4 * HALF_ROWS + (2 * half + low) * 2 * ALONG
    return wide_rows(tables, start, 2 * ALONG)


def extra_rows(tables, half):
    start = 4 * HALF_ROWS + 8 * ALONG
    return tables[half, start : start + ALONG, :]


def depth_table():
    theta = angles(np.arange(DEPTH), np.arange(DEPTH), DEPTH).reshape(DEPTH, SUBS, LOCAL)
    table = np.zeros((2, 2, DEPTH, SUBS, 2, LOCAL))
    for half in range(2):
        table[0, half, :, :, half, :] = np.cos(theta)
        table[1, half, :, :, half, :] = np.sin(theta)
    return table.reshape(4 * DEPTH, 2 * DEPTH)


def window_table():
    freq = np.arange(DEPTH)
    table = np.zeros((OFFS, 6, 16, DEPTH))
    low, high = (freq >= 1) & (freq < 64), freq > 64
    for index in range(OFFS):
        steps = np.arange(WIN) - REACH + index - MAX_OFF
        theta = angles(steps, freq, DEPTH)
        cos, sin = np.cos(theta), np.sin(theta)
        edge = 0.5 * cos * ((freq == 0) | (freq == 64))
        table[index, 0, :WIN] = cos
        table[index, 1, :WIN] = sin
        table[index, 2, :WIN] = cos * low + edge
        table[index, 3, :WIN] = sin * low
        table[index, 4, :WIN] = cos * high
        table[index, 5, :WIN] = edge - sin * high
    return table.reshape(OFFS, 96, DEPTH)


def step_table():
    step = np.arange(WIN) - REACH
    table = np.zeros((2, 2, HALF, 128))
    for half in range(2):
        theta = angles(np.arange(HALF) + half, step, ALONG)
        table[half, 0, :, :WIN] = np.cos(theta)
        table[half, 1, :, :WIN] = -np.sin(theta)
        table[half, 0, :, 64 : 64 + WIN] = np.sin(theta)
        table[half, 1, :, 64 : 64 + WIN] = np.cos(theta)
    high, low = split_np(table.reshape(2, 2 * HALF, 128) * (2.0 / VOXELS))
    return np.stack([high, low], axis=1)


def turn_table():
    step = np.arange(WIN) - REACH
    table = np.zeros((SUBS, 16, 128), np.float32)
    for sub in range(SUBS):
        theta = angles(step, [sub], ACROSS)
        table[sub, :WIN, :64] = np.cos(theta)
        table[sub, :WIN, 64:] = -np.sin(theta)
    table[0, :WIN, 64:] = np.where(step % 2 == 0, 1.0, -1.0)[:, None]
    return table


def shift_table():
    table = np.zeros((2, 2, 16, HALF))
    for half in range(2):
        theta = angles(np.arange(OFFS) - MAX_OFF, np.arange(HALF) + half, ALONG)
        table[half, 0, :OFFS] = np.cos(theta)
        table[half, 1, :OFFS] = np.sin(theta)
    return table.reshape(4, 16, HALF).astype(np.float32)


GROUP = 6


def place_table():
    table = np.zeros((3, 4, 8, 128), np.float32)
    for index in range(4 * WIN):
        pair, depth = divmod(index, WIN)
        group, row = divmod(index, GROUP)
        for along in range(WIN):
            table[:, pair, row, WIN * group + along] = (1.0, depth - REACH, along - REACH)
    return table


def circle_table():
    theta = np.arange(ACROSS) * (2.0 * np.pi / ACROSS)
    return np.stack([np.cos(theta), np.sin(theta)]).astype(np.float32)


def graph_table():
    table = np.zeros((PLANES, 8, ROW * PLANES), np.float32)
    for plane in range(PLANES):
        base = ROW * plane
        pairs = [(base, base + 1), (base + 2, base + 3), (base + 1, base + 2)]
        pairs += [(base - ROW + col, base + col) for col in range(ROW)]
        for slot, (first, second) in enumerate(pairs):
            if first >= 0:
                table[plane, slot, first] = 1.0
                table[plane, slot, second] = -1.0
    return table.reshape(PLANES * 8, ROW * PLANES)


def dot(left, right):
    return jnp.dot(left, right, preferred_element_type=F32)


def split(value):
    high = value.astype(BF)
    return high, (value - high.astype(F32)).astype(BF)


def across_dft(strip, half, tables):
    both = dot(across_rows(tables, half, 0), strip) + dot(across_rows(tables, half, 1), strip)
    rows = SUBS * LOCAL
    return jnp.concatenate([both[:rows], both[rows:]], axis=1)


def along_dft(value, half, tables, count):
    high, low = split(value)
    table_hi, table_lo = along_rows(tables, half, 0), along_rows(tables, half, 1)
    out = dot(high, table_hi) + dot(low, table_hi) + dot(high, table_lo)
    extra = extra_rows(tables, half)
    rows = SUBS * LOCAL
    edge_hi = jnp.concatenate([high[rows * k : rows * k + 16, :ALONG] for k in range(count)], axis=0)
    edge_lo = jnp.concatenate([low[rows * k : rows * k + 16, :ALONG] for k in range(count)], axis=0)
    more = dot(edge_hi, extra) + dot(edge_lo, extra)
    pieces = []
    for k in range(count):
        block = out[rows * k : rows * (k + 1)]
        head = block[:LOCAL]
        head = jnp.concatenate(
            [head[:, :HALF], head[:, HALF:] + more[16 * k : 16 * k + LOCAL]], axis=1
        )
        pieces.append(jnp.concatenate([head, block[LOCAL:]], axis=0).reshape(SUBS, LOCAL, 2 * HALF))
    return pieces


def pair_facts(where, pair_tiles, owner, pair_offset):
    plane, core = where[0], where[1]
    base = ROW * plane
    count = owner.shape[1]
    row = lax.broadcasted_iota(jnp.int32, (16, count), 0)
    place = lax.broadcasted_iota(jnp.int32, (16, count), 1)
    home = 2 * base + jnp.where(row == 1, 4, jnp.where(row == 2, 2, 0))
    up = 2 * (base - ROW + row - 3) + 1
    down = 2 * (base + 2 * core + row - 7) + 1
    wanted = jnp.where(row < 3, home, jnp.where(row < 7, up, jnp.where(row < 9, down, -100)))
    first, second = pair_tiles[0:1, :], pair_tiles[1:2, :]
    key = first * 2 + jnp.where(second - first == 1, 0, 1)
    match = wanted == key
    owned = jnp.broadcast_to(owner[...] == 2 * plane + core, match.shape)

    def total(mask, value):
        return jnp.sum(jnp.where(mask, value, 0), axis=1, keepdims=True)

    offset = [total(match, jnp.broadcast_to(pair_offset[k : k + 1, :], match.shape)) for k in range(3)]
    at = total(match, place)
    held = total(match & owned, 1)
    ordinal = total((place < at) & owned, 1)
    return offset, jnp.where(held > 0, ordinal, -1)


def facts_kernel(where, pair_tiles, owner, pair_offset, ignored, facts, offsets):
    del ignored
    offset, slot = pair_facts(where, pair_tiles, owner, pair_offset)
    lane = lax.broadcasted_iota(jnp.int32, (16, 128), 1)
    facts[...] = jnp.where(
        lane == 0, offset[0], jnp.where(lane == 1, offset[1], jnp.where(lane == 2, offset[2], slot))
    )
    lane = lane[:8]
    offsets[...] = jnp.where(
        lane == 1, offset[0][:8], jnp.where(lane == 2, offset[1][:8], offset[2][:8])
    ).astype(F32)


def chunk(pieces):
    return jnp.concatenate(pieces, axis=1).astype(BF)


def local_kernel(where, strips, own, other, tables, out):
    chosen = (1, 4, 2, 6)
    parts = []
    for half in range(2):
        stack = [across_dft(strips[k], half, tables) for k in chosen]
        parts.append(along_dft(jnp.concatenate(stack, axis=0), half, tables, 4))
    for k in range(4):
        out[:, 16 * k : 16 * k + 16, :] = chunk([parts[0][k], parts[1][k]])
    core = where[1]
    mine, theirs = own[...], other[...]
    first = jnp.where(core == 0, mine, theirs)
    second = jnp.where(core == 0, theirs, mine)
    stack = [across_dft(strip, core, tables) for strip in (first, second)]
    out[:, 96:112, :] = chunk(along_dft(jnp.concatenate(stack, axis=0), core, tables, 2))


def remote_kernel(here, below, tables, ignored, out, moved):
    del ignored
    kept = ((pl.ds(0, 16), pl.ds(0, 64)), (pl.ds(0, 16), pl.ds(96, 16)))
    copies = [
        pltpu.make_async_copy(here.at[at + (slice(None),)], out.at[at + (slice(None),)], moved.at[k])
        for k, at in enumerate(kept)
    ]
    for copy in copies:
        copy.start()
    parts = []
    for half in range(2):
        stack = [across_dft(below[k], half, tables) for k in range(2)]
        parts.append(along_dft(jnp.concatenate(stack, axis=0), half, tables, 2))
    for k in range(2):
        out[:, 64 + 16 * k : 80 + 16 * k, :] = chunk([parts[0][k], parts[1][k]])
    for copy in copies:
        copy.wait()


def spectrum_of(block, lanes, depth_hi, depth_lo):
    both = dot(depth_hi, block) + dot(depth_lo, block)
    cos, sin = both[: 2 * DEPTH], both[2 * DEPTH :]
    cos_re, cos_im = cos[:, :HALF], cos[:, HALF:]
    sin_re, sin_im = sin[:, :HALF], sin[:, HALF:]
    real, imag = cos_re + sin_im, cos_im - sin_re
    if lanes is not None:
        low, high = lanes
        real = jnp.where(low, cos_re, jnp.where(high, cos_im, real))
        imag = jnp.where(low, -sin_re, jnp.where(high, -sin_im, imag))
    return real, imag


def phase_of(first, second, edge):
    floor = (FLOOR_SHARE * VOXELS) ** 2
    first_re, first_im = first
    second_re, second_im = second
    straight, crossed = first_re * second_re, first_im * second_im
    imag = first_im * second_re - first_re * second_im
    if edge is None:
        real = straight + crossed
        norm = lax.rsqrt(real * real + imag * imag + floor)
        return real * norm, imag * norm
    real = straight + jnp.where(edge, 0.0, crossed)
    imag = jnp.where(edge, crossed, imag)
    real_sq, imag_sq = real * real, imag * imag
    norm = lax.rsqrt(real_sq + jnp.where(edge, 0.0, imag_sq) + floor)
    norm_im = jnp.where(edge, lax.rsqrt(imag_sq + floor), norm)
    return real * norm, imag * norm_im


def window_kernel(where, meta, circle, got, depth, vhi, vlo, steps, shift, out):
    c, d = where[1], where[2]
    row = lax.broadcasted_iota(jnp.int32, (2 * DEPTH, HALF), 0)
    lane = lax.broadcasted_iota(jnp.int32, (2 * DEPTH, HALF), 1)
    freq = lax.rem(row, DEPTH)
    nowhere = jnp.where(d == 0, 0, 2 * HALF)

    def special(half_of_row):
        held = lane == half_of_row * (HALF - 1) + nowhere
        low = held & (freq > 0) & (freq < 64)
        high = held & (freq > 64)
        edge = held & ((freq == 0) | (freq == 64))
        return (low, high), edge

    lanes, edge = special(row // DEPTH)
    depth_hi, depth_lo = wide_rows(depth, 0, 512), wide_rows(depth, 512, 512)

    def spectrum(slot, masks):
        block = got[:, 16 * slot : 16 * slot + 16, :].reshape(2 * DEPTH, 2 * HALF)
        return spectrum_of(block, masks, depth_hi, depth_lo)

    small_lane = lax.broadcasted_iota(jnp.int32, (16, HALF), 1)

    def window_rows(phase, half, slot):
        off_z, off_y, off_x = meta[slot, 0], meta[slot, 1], meta[slot, 2]
        high, low = split(jnp.concatenate(phase, axis=1))
        table_hi, table_lo = vhi[off_z + MAX_OFF], vlo[off_z + MAX_OFF]
        rows = dot(table_hi, high) + dot(table_lo, high) + dot(table_hi, low)
        part = [(rows[16 * k : 16 * k + 16, :HALF], rows[16 * k : 16 * k + 16, HALF:]) for k in range(6)]
        held = small_lane == half * (HALF - 1) + nowhere
        real = jnp.where(held, part[2][0] - part[3][1], part[0][0] - part[1][1])
        imag = jnp.where(held, 0.0, part[1][0] + part[0][1])
        freq_y = jnp.where(half == 0, d, jnp.where(d == 0, ACROSS // 2, ACROSS - d))
        turn = lax.rem(freq_y * (off_y + ACROSS), ACROSS)
        cos_y, sin_y = circle[0, turn], circle[1, turn]
        cos_x = shift[2 * half, pl.ds(off_x + MAX_OFF, 1), :]
        sin_x = shift[2 * half + 1, pl.ds(off_x + MAX_OFF, 1), :]
        cos = cos_x * cos_y - sin_x * sin_y
        sin = sin_x * cos_y + cos_x * sin_y
        turned = jnp.concatenate([real * cos - imag * sin, real * sin + imag * cos], axis=1)
        other = jnp.sum(jnp.where(held, part[4][0] + part[5][1], 0.0), axis=1, keepdims=True)
        even = (lax.rem(small_lane + off_x + 6, 2) == 0) | (half == 1)
        sign = jnp.where(even, 1.0, -1.0) * (cos_y * (2.0 / VOXELS))
        return turned, other * jnp.where(small_lane < WIN, sign, 0.0)

    terms, extra = ([], []), ([], [])
    for first, second, slot in ((0, 1, c), (4, 2, 3 + 2 * c), (5, 3, 4 + 2 * c)):
        real, imag = phase_of(spectrum(first, lanes), spectrum(second, lanes), edge)
        for half in range(2):
            rows = slice(DEPTH * half, DEPTH * (half + 1))
            turned, more = window_rows((real[rows], imag[rows]), half, slot)
            terms[half].append(turned)
            extra[half].append(more)
    seam_lanes, seam_edge = special(c)
    real, imag = spectrum(6, seam_lanes)
    phase = phase_of(
        (real[:DEPTH], imag[:DEPTH]), (real[DEPTH:], imag[DEPTH:]), seam_edge[:DEPTH]
    )
    turned, more = window_rows(phase, c, 2)
    for half in range(2):
        terms[half].append(jnp.where(c == half, turned, 0.0))
        extra[half].append(jnp.where(c == half, more, 0.0))
    sums = []
    for half in range(2):
        high, low = split(jnp.concatenate(terms[half], axis=0))
        table_hi, table_lo = steps[half, 0], steps[half, 1]
        total = dot(high, table_hi) + dot(low, table_hi) + dot(high, table_lo)
        sums.append(total + jnp.concatenate(extra[half], axis=0))
    lane = lax.broadcasted_iota(jnp.int32, sums[0].shape, 1)
    both = sums[0] + jnp.where(lane < 64, sums[1], -sums[1])
    apart = jnp.where(lane < 64, sums[0], pltpu.roll(sums[1], 64, 1))
    both = jnp.where(d == 0, apart, both)
    rows = jnp.concatenate([both[16 * k : 16 * k + WIN] for k in range(4)], axis=0)
    packed = rows[:GROUP]
    for group in range(1, GROUP):
        packed = packed + pltpu.roll(rows[GROUP * group : GROUP * (group + 1)], WIN * group, 1)
    packed = jnp.concatenate([packed, jnp.zeros((2, 128), F32)], axis=0)
    out[...] = jnp.broadcast_to(packed[None], out.shape)


def energy_kernel(where, got, offsets, turns, places, windows, terms):
    sums = [[None] * WIN, [None] * WIN]
    for sub in range(SUBS):
        turn = turns[sub]
        for core in range(2):
            value = got[SUBS * core + sub]
            for step in range(WIN):
                term = value * turn[step : step + 1]
                sums[core][step] = term if sub == 0 else sums[core][step] + term
    sums = [[value + pltpu.roll(value, 64, 1) for value in side] for side in sums]
    seam = [left + right for left, right in zip(*sums)]
    totals = []
    for side in (sums[0], sums[1], seam):
        squares = [value * value for value in side]
        total = squares[0]
        for value in squares[1:]:
            total = total + value
        across = squares[0] * float(-REACH)
        for step in range(1, WIN):
            across = across + squares[step] * float(step - REACH)
        totals.append((total, across))
    slots = ((0, 0), (1, 0), (2, 3), (0, 1), (0, 2), (1, 1), (1, 2))

    def stacked(kind, which):
        rows = [
            jnp.sum(totals[side][which] * places[kind, pair], axis=0, keepdims=True)
            for side, pair in slots
        ]
        rows = jnp.concatenate(rows + [jnp.zeros((1, 128), F32)], axis=0)
        return jnp.sum(rows, axis=1, keepdims=True)

    energy = stacked(0, 0)
    moments = [stacked(1, 0), stacked(0, 1), stacked(2, 0)]
    lane = lax.broadcasted_iota(jnp.int32, (8, 128), 1)
    mixed = jnp.where(lane == 1, moments[0], jnp.where(lane == 2, moments[1], moments[2]))
    place = offsets[...] + mixed / (energy + EPSILON)
    value = jnp.where(lane == 0, energy, energy * place)
    value = jnp.where(lane < 4, value, 0.0)
    terms[...] = jnp.broadcast_to(value[None], terms.shape)
    is_left = where[1] == 0
    at_seam = places[0, 3] > 0.0
    for step in range(WIN):
        mine = jnp.where(is_left, sums[0][step], sums[1][step])
        windows[step] = jnp.where(at_seam, seam[step], mine)


def unpack(packed):
    lane = lax.broadcasted_iota(jnp.int32, (8, 128), 1)
    values = [packed[step] for step in range(WIN)]
    groups = []
    for group in range(GROUP):
        inside = (lane >= WIN * group) & (lane < WIN * (group + 1))
        rows = jnp.zeros((8, 128), F32)
        for step in range(WIN):
            moved = WIN * (step - group) % 128
            value = jnp.where(inside, values[step], 0.0)
            rows = rows + (pltpu.roll(value, moved, 1) if moved else value)
        groups.append(rows[:GROUP])
    rows = jnp.concatenate(groups, axis=0)
    return [rows[WIN * pair : WIN * (pair + 1)] for pair in range(4)]


def graph_kernel(terms, graph, ignored, matrix, rhs):
    del ignored
    table = graph[...]
    value = terms[...].reshape(PLANES * 8, 128)
    weighted = table * value[:, :1]
    over = (((0,), (0,)), ((), ()))
    matrix[...] = lax.dot_general(
        table, weighted, over, precision=lax.Precision.HIGHEST, preferred_element_type=F32
    )
    load = lax.dot_general(
        value, table, over, precision=lax.Precision.HIGHEST, preferred_element_type=F32
    )
    rhs[...] = load[1:4]


def place_kernel(where, meta, mine, below, windows, done):
    done[...] = mine[0]
    c = where[1]
    slot = lax.broadcasted_iota(jnp.int32, (6, 128), 0)
    blocks = unpack(mine) + unpack(below)[1:3]
    places = [slot == meta[k, 3] for k in (c, 3 + 2 * c, 4 + 2 * c, 2, 7, 8)]
    for step in range(WIN):
        rows = jnp.zeros((6, 128), F32)
        for block, place in zip(blocks, places):
            rows = jnp.where(place, block[step : step + 1], rows)
        windows[:, WIN * WIN * step : WIN * WIN * (step + 1)] = rows[:, : WIN * WIN]


def call(kernel, shapes, operands, spaces, **params):
    specs = [pl.BlockSpec(memory_space=space) for space in spaces]
    outs = jax.tree.map(lambda _: pl.BlockSpec(memory_space=pltpu.VMEM), shapes)
    return pl.pallas_call(
        kernel,
        out_shape=shapes,
        in_specs=specs,
        out_specs=outs,
        compiler_params=pltpu.CompilerParams(vmem_limit_bytes=16 * 1024 * 1024),
        **params,
    )(*operands)


def local(strips, pair_tiles, pair_owner, pair_offset):
    where = jnp.stack([lax.axis_index(name) for name in ("z", "core", "sub")]).astype(jnp.int32)
    tables = plane_dft_tables()
    depth = lane_tiles(np.concatenate(split_np(depth_table()), axis=0))
    vhi, vlo = split_np(window_table())
    vmem, smem = pltpu.VMEM, pltpu.SMEM

    tiles = strips.reshape(8, LOCAL * ACROSS, ALONG)
    bottoms = jnp.stack([tiles[3], tiles[7]])
    from_above = lax.ppermute(bottoms, "z", [(k, k + 1) for k in range(PLANES - 1)])
    core, bottoms = lax.optimization_barrier((where[1], bottoms))
    own = lax.dynamic_index_in_dim(tiles, 5 - 5 * core, 0, keepdims=False)
    other = lax.ppermute(own, "core", [(0, 1), (1, 0)])

    chunks = jax.ShapeDtypeStruct((SUBS, 112, 2 * HALF), BF)
    here = call(
        local_kernel,
        chunks,
        (where, tiles, own, other, tables),
        (smem,) + (vmem,) * 4,
    )
    facts, offsets = call(
        facts_kernel,
        (jax.ShapeDtypeStruct((16, 128), jnp.int32), jax.ShapeDtypeStruct((8, 128), F32)),
        (where, pair_tiles.T, pair_owner.reshape(1, -1), pair_offset.T, here),
        (smem,) + (vmem,) * 3 + (pl.ANY,),
    )
    sent = call(
        remote_kernel,
        chunks,
        (here, from_above, tables, offsets),
        (vmem,) * 3 + (pl.ANY,),
        scratch_shapes=[pltpu.SemaphoreType.DMA((2,))],
    )
    got = lax.all_to_all(sent, "sub", split_axis=0, concat_axis=0, tiled=True)
    partial = call(
        window_kernel,
        jax.ShapeDtypeStruct((2 * SUBS, 8, 128), F32),
        (where, facts, circle_table(), got, depth, vhi, vlo, step_table(), shift_table()),
        (smem,) * 3 + (vmem,) * 6,
    )
    shares = lax.all_to_all(partial, ("core", "sub"), split_axis=0, concat_axis=0, tiled=True)
    mine, terms = call(
        energy_kernel,
        (jax.ShapeDtypeStruct((WIN, 8, 128), F32), jax.ShapeDtypeStruct((PLANES, 8, 128), F32)),
        (where, shares, offsets, turn_table(), place_table()),
        (smem, vmem, vmem, vmem, vmem),
    )
    below = lax.ppermute(mine, "z", [(k + 1, k) for k in range(PLANES - 1)])
    all_terms = lax.all_to_all(terms, "z", split_axis=0, concat_axis=0, tiled=True)
    windows, done = call(
        place_kernel,
        (jax.ShapeDtypeStruct((6, WIN * WIN * WIN), F32), jax.ShapeDtypeStruct((8, 128), F32)),
        (where, facts, mine, below),
        (smem, smem, vmem, vmem),
    )
    matrix, rhs = call(
        graph_kernel,
        (jax.ShapeDtypeStruct((64, 64), F32), jax.ShapeDtypeStruct((3, 64), F32)),
        (all_terms, graph_table(), done),
        (vmem, vmem, pl.ANY),
    )
    return windows, matrix, rhs.T


def solution(mesh):
    grid = Mesh(mesh.devices.reshape(PLANES, 2, SUBS), ("z", "core", "sub"))
    tiles = ("z", "core")
    in_specs = (P(tiles, None, "sub", None, None), P(), P(), P())
    out_specs = (P(tiles, None), P(), P())
    return jax.shard_map(local, mesh=grid, in_specs=in_specs, out_specs=out_specs, check_vma=False)
```

```python
import jax
import jax.numpy as jnp
import ml_dtypes
import numpy as np
from jax import lax
from jax.experimental import pallas as pl
from jax.experimental.pallas import tpu as pltpu
from jax.sharding import Mesh, PartitionSpec as P

REACH = 4
WIN = 9
EPSILON = 1e-06
FLOOR_SHARE = 0.05
ROW = 4
PLANES = 16
SUBS = 16
DEPTH, ACROSS, ALONG = 128, 32, 256
LOCAL = DEPTH // SUBS
HALF = ALONG // 2
VOXELS = DEPTH * ACROSS * ALONG
MAX_OFF = 5
OFFS = 2 * MAX_OFF + 1
BF = jnp.bfloat16
F32 = jnp.float32


def split_np(table):
    high = table.astype(ml_dtypes.bfloat16)
    low = (table - high.astype(np.float64)).astype(ml_dtypes.bfloat16)
    return high, low


def lane_tiles(table):
    return np.stack([table[..., :128], table[..., 128:]], axis=-3)


def angles(rows, cols, length):
    return (np.outer(rows, cols) % length) * (2.0 * np.pi / length)


def across_freq(half, sub):
    if half == 0:
        return sub
    return ACROSS // 2 if sub == 0 else ACROSS - sub


def across_table():
    table = np.zeros((2, 2, SUBS, LOCAL, LOCAL, ACROSS))
    for half in range(2):
        for sub in range(SUBS):
            theta = angles([across_freq(half, sub)], np.arange(ACROSS), ACROSS)[0]
            for plane in range(LOCAL):
                table[half, 0, sub, plane, plane] = np.cos(theta)
                table[half, 1, sub, plane, plane] = -np.sin(theta)
    return table.reshape(2, 2 * SUBS * LOCAL, LOCAL * ACROSS)


def along_table():
    table = np.zeros((2, 2, ALONG, 2, HALF))
    for half in range(2):
        theta = angles(np.arange(ALONG), np.arange(HALF) + half, ALONG)
        table[half, 0, :, 0] = np.cos(theta)
        table[half, 0, :, 1] = -np.sin(theta)
        table[half, 1, :, 0] = np.sin(theta)
        table[half, 1, :, 1] = np.cos(theta)
    return table.reshape(2, 2 * ALONG, 2 * HALF)


def extra_table():
    table = np.zeros((2, ALONG, HALF))
    table[0, :, 0] = np.where(np.arange(ALONG) % 2 == 0, 1.0, -1.0)
    table[1, :, HALF - 1] = 1.0
    return table


HALF_ROWS = 2 * SUBS * LOCAL


def plane_dft_tables():
    across, along = split_np(across_table()), split_np(along_table())
    extra = extra_table().astype(ml_dtypes.bfloat16)
    pieces = [part[half] for half in range(2) for part in across]
    pieces += [part[half] for half in range(2) for part in along]
    pieces.append(np.concatenate([extra[0], extra[1]], axis=1))
    return lane_tiles(np.concatenate(pieces, axis=0))


def wide_rows(tables, start, count):
    rows = pl.ds(pl.multiple_of(start, 256), count)
    return jnp.concatenate([tables[0, rows, :], tables[1, rows, :]], axis=1)


def across_rows(tables, half, low):
    return wide_rows(tables, (2 * half + low) * HALF_ROWS, HALF_ROWS)


def along_rows(tables, half, low):
    start = 4 * HALF_ROWS + (2 * half + low) * 2 * ALONG
    return wide_rows(tables, start, 2 * ALONG)


def extra_rows(tables, half):
    start = 4 * HALF_ROWS + 8 * ALONG
    return tables[half, start : start + ALONG, :]


def depth_table():
    theta = angles(np.arange(64), np.arange(DEPTH), DEPTH)
    cos, sin = np.cos(theta), np.sin(theta)
    sin[0] = np.where(np.arange(DEPTH) % 2 == 0, 1.0, -1.0)
    table = np.zeros((2, 2, 64, SUBS, 2, LOCAL))
    for half in range(2):
        table[0, half, :, :, half, :] = cos.reshape(64, SUBS, LOCAL)
        table[1, half, :, :, half, :] = sin.reshape(64, SUBS, LOCAL)
    return table.reshape(4 * 64, 2 * DEPTH)


ORDER = np.concatenate([np.arange(65), np.arange(127, 64, -1)])


def window_table():
    freq = np.arange(DEPTH)
    table = np.zeros((OFFS, 6, 16, DEPTH))
    low, high = (freq >= 1) & (freq < 64), freq > 64
    for index in range(OFFS):
        steps = np.arange(WIN) - REACH + index - MAX_OFF
        theta = angles(steps, freq, DEPTH)
        cos, sin = np.cos(theta), np.sin(theta)
        edge = 0.5 * cos * ((freq == 0) | (freq == 64))
        table[index, 0, :WIN] = cos
        table[index, 1, :WIN] = sin
        table[index, 2, :WIN] = cos * low + edge
        table[index, 3, :WIN] = sin * low
        table[index, 4, :WIN] = cos * high
        table[index, 5, :WIN] = edge - sin * high
    return table.reshape(OFFS, 96, DEPTH)[:, :, ORDER]


def step_table():
    step = np.arange(WIN) - REACH
    table = np.zeros((2, 2, HALF, 128))
    for half in range(2):
        theta = angles(np.arange(HALF) + half, step, ALONG)
        table[half, 0, :, :WIN] = np.cos(theta)
        table[half, 1, :, :WIN] = -np.sin(theta)
        table[half, 0, :, 64 : 64 + WIN] = np.sin(theta)
        table[half, 1, :, 64 : 64 + WIN] = np.cos(theta)
    high, low = split_np(table.reshape(2, 2 * HALF, 128) * (2.0 / VOXELS))
    return np.stack([high, low], axis=1)


def turn_table():
    step = np.arange(WIN) - REACH
    table = np.zeros((SUBS, 16, 128), np.float32)
    for sub in range(SUBS):
        theta = angles(step, [sub], ACROSS)
        table[sub, :WIN, :64] = np.cos(theta)
        table[sub, :WIN, 64:] = -np.sin(theta)
    table[0, :WIN, 64:] = np.where(step % 2 == 0, 1.0, -1.0)[:, None]
    return table


def shift_table():
    table = np.zeros((2, 2, 16, HALF))
    for half in range(2):
        theta = angles(np.arange(OFFS) - MAX_OFF, np.arange(HALF) + half, ALONG)
        table[half, 0, :OFFS] = np.cos(theta)
        table[half, 1, :OFFS] = np.sin(theta)
    return table.reshape(4, 16, HALF).astype(np.float32)


GROUP = 6


def place_table():
    table = np.zeros((3, 4, 8, 128), np.float32)
    for index in range(4 * WIN):
        pair, depth = divmod(index, WIN)
        group, row = divmod(index, GROUP)
        for along in range(WIN):
            table[:, pair, row, WIN * group + along] = (1.0, depth - REACH, along - REACH)
    return table


def circle_table():
    theta = np.arange(ACROSS) * (2.0 * np.pi / ACROSS)
    return np.stack([np.cos(theta), np.sin(theta)]).astype(np.float32)


def graph_table():
    table = np.zeros((PLANES, 8, ROW * PLANES), np.float32)
    for plane in range(PLANES):
        base = ROW * plane
        pairs = [(base, base + 1), (base + 2, base + 3), (base + 1, base + 2)]
        pairs += [(base - ROW + col, base + col) for col in range(ROW)]
        for slot, (first, second) in enumerate(pairs):
            if first >= 0:
                table[plane, slot, first] = 1.0
                table[plane, slot, second] = -1.0
    return table.reshape(PLANES * 8, ROW * PLANES)


def dot(left, right):
    return jnp.dot(left, right, preferred_element_type=F32)


def split(value):
    high = value.astype(BF)
    return high, (value - high.astype(F32)).astype(BF)


def across_dft(strip, half, tables):
    both = dot(across_rows(tables, half, 0), strip) + dot(across_rows(tables, half, 1), strip)
    rows = SUBS * LOCAL
    return jnp.concatenate([both[:rows], both[rows:]], axis=1)


def along_dft(value, half, tables, count):
    high, low = split(value)
    table_hi, table_lo = along_rows(tables, half, 0), along_rows(tables, half, 1)
    out = dot(high, table_hi) + dot(low, table_hi) + dot(high, table_lo)
    extra = extra_rows(tables, half)
    rows = SUBS * LOCAL
    edge_hi = jnp.concatenate([high[rows * k : rows * k + 16, :ALONG] for k in range(count)], axis=0)
    edge_lo = jnp.concatenate([low[rows * k : rows * k + 16, :ALONG] for k in range(count)], axis=0)
    more = dot(edge_hi, extra) + dot(edge_lo, extra)
    pieces = []
    for k in range(count):
        block = out[rows * k : rows * (k + 1)]
        head = block[:LOCAL]
        head = jnp.concatenate(
            [head[:, :HALF], head[:, HALF:] + more[16 * k : 16 * k + LOCAL]], axis=1
        )
        pieces.append(jnp.concatenate([head, block[LOCAL:]], axis=0).reshape(SUBS, LOCAL, 2 * HALF))
    return pieces


def pair_facts(where, pair_tiles, owner, pair_offset):
    plane, core = where[0], where[1]
    base = ROW * plane
    count = owner.shape[1]
    row = lax.broadcasted_iota(jnp.int32, (16, count), 0)
    place = lax.broadcasted_iota(jnp.int32, (16, count), 1)
    home = 2 * base + jnp.where(row == 1, 4, jnp.where(row == 2, 2, 0))
    up = 2 * (base - ROW + row - 3) + 1
    down = 2 * (base + 2 * core + row - 7) + 1
    wanted = jnp.where(row < 3, home, jnp.where(row < 7, up, jnp.where(row < 9, down, -100)))
    first, second = pair_tiles[0:1, :], pair_tiles[1:2, :]
    key = first * 2 + jnp.where(second - first == 1, 0, 1)
    match = wanted == key
    owned = jnp.broadcast_to(owner[...] == 2 * plane + core, match.shape)

    def total(mask, value):
        return jnp.sum(jnp.where(mask, value, 0), axis=1, keepdims=True)

    offset = [total(match, jnp.broadcast_to(pair_offset[k : k + 1, :], match.shape)) for k in range(3)]
    at = total(match, place)
    held = total(match & owned, 1)
    ordinal = total((place < at) & owned, 1)
    return offset, jnp.where(held > 0, ordinal, -1)


def chunk(pieces):
    return jnp.concatenate(pieces, axis=1).astype(BF)


def local_kernel(strips, tables, out):
    chosen = (1, 4, 2, 6)
    parts = []
    for half in range(2):
        stack = [across_dft(strips[k], half, tables) for k in chosen]
        parts.append(along_dft(jnp.concatenate(stack, axis=0), half, tables, 4))
    for k in range(4):
        out[:, 16 * k : 16 * k + 16, :] = chunk([parts[0][k], parts[1][k]])


def remote_kernel(
    where, here, below, own, other, tables, pair_tiles, owner, pair_offset,
    out, facts, offsets, moved,
):
    kept = pltpu.make_async_copy(here, out.at[:, pl.ds(0, 64), :], moved)
    kept.start()
    offset, slot = pair_facts(where, pair_tiles, owner, pair_offset)
    lane = lax.broadcasted_iota(jnp.int32, (16, 128), 1)
    facts[...] = jnp.where(
        lane == 0, offset[0], jnp.where(lane == 1, offset[1], jnp.where(lane == 2, offset[2], slot))
    )
    lane = lane[:8]
    offsets[...] = jnp.where(
        lane == 1, offset[0][:8], jnp.where(lane == 2, offset[1][:8], offset[2][:8])
    ).astype(F32)
    parts = []
    for half in range(2):
        stack = [across_dft(below[k], half, tables) for k in range(2)]
        parts.append(along_dft(jnp.concatenate(stack, axis=0), half, tables, 2))
    for k in range(2):
        out[:, 64 + 16 * k : 80 + 16 * k, :] = chunk([parts[0][k], parts[1][k]])
    core = where[1]
    mine, theirs = own[...], other[...]
    first = jnp.where(core == 0, mine, theirs)
    second = jnp.where(core == 0, theirs, mine)
    stack = [across_dft(strip, core, tables) for strip in (first, second)]
    out[:, 96:112, :] = chunk(along_dft(jnp.concatenate(stack, axis=0), core, tables, 2))
    kept.wait()


def spectrum_of(block, zeroth, held, depth_hi, depth_lo):
    both = dot(depth_hi, block) + dot(depth_lo, block)
    cos, sin = both[:DEPTH], both[DEPTH:]
    cos_re, cos_im = cos[:, :HALF], cos[:, HALF:]
    sin_re, sin_im = sin[:, :HALF], sin[:, HALF:]
    low_re = jnp.where(zeroth | held, cos_re, cos_re + sin_im)
    low_im = jnp.where(zeroth, cos_im, jnp.where(held, 0.0, cos_im) - sin_re)
    high_re = jnp.where(zeroth, sin_re, jnp.where(held, cos_im, cos_re - sin_im))
    high_im = jnp.where(zeroth, sin_im, jnp.where(held, sin_im, cos_im + sin_re))

    def rows(low, high):
        return jnp.concatenate([low[:64], high[:64], low[64:], high[64:]], axis=0)

    return rows(low_re, high_re), rows(low_im, high_im)


def phase_of(first, second, edge):
    floor = (FLOOR_SHARE * VOXELS) ** 2
    first_re, first_im = first
    second_re, second_im = second
    straight, crossed = first_re * second_re, first_im * second_im
    imag = first_im * second_re - first_re * second_im
    if edge is None:
        real = straight + crossed
        norm = lax.rsqrt(real * real + imag * imag + floor)
        return real * norm, imag * norm
    real = straight + jnp.where(edge, 0.0, crossed)
    imag = jnp.where(edge, crossed, imag)
    real_sq, imag_sq = real * real, imag * imag
    norm = lax.rsqrt(real_sq + jnp.where(edge, 0.0, imag_sq) + floor)
    norm_im = jnp.where(edge, lax.rsqrt(imag_sq + floor), norm)
    return real * norm, imag * norm_im


def window_kernel(where, meta, circle, got, depth, vhi, vlo, steps, shift, out):
    c, d = where[1], where[2]
    row = lax.broadcasted_iota(jnp.int32, (DEPTH, HALF), 0)
    lane = lax.broadcasted_iota(jnp.int32, (DEPTH, HALF), 1)
    zeroth = lax.rem(row, 64) == 0
    nowhere = jnp.where(d == 0, 0, 2 * HALF)

    def special(half_of_row):
        return (lane == half_of_row * (HALF - 1) + nowhere) & (lax.rem(row, 64) != 0)

    def edges(count, half_of_row):
        row = lax.broadcasted_iota(jnp.int32, (count, HALF), 0)
        lane = lax.broadcasted_iota(jnp.int32, (count, HALF), 1)
        return (lane == half_of_row(row) * (HALF - 1) + nowhere) & (lax.rem(row, 64) == 0)

    held = special(row // 64)
    edge = edges(2 * DEPTH, lambda row: row // DEPTH)
    depth_hi, depth_lo = wide_rows(depth, 0, 256), wide_rows(depth, 256, 256)

    def spectrum(slot, held):
        block = got[:, 16 * slot : 16 * slot + 16, :].reshape(2 * DEPTH, 2 * HALF)
        return spectrum_of(block, zeroth, held, depth_hi, depth_lo)

    small_lane = lax.broadcasted_iota(jnp.int32, (16, HALF), 1)

    def window_rows(phase, half, slot):
        off_z, off_y, off_x = meta[slot, 0], meta[slot, 1], meta[slot, 2]
        high, low = split(jnp.concatenate(phase, axis=1))
        table_hi, table_lo = vhi[off_z + MAX_OFF], vlo[off_z + MAX_OFF]
        rows = dot(table_hi, high) + dot(table_lo, high) + dot(table_hi, low)
        part = [(rows[16 * k : 16 * k + 16, :HALF], rows[16 * k : 16 * k + 16, HALF:]) for k in range(6)]
        held = small_lane == half * (HALF - 1) + nowhere
        real = jnp.where(held, part[2][0] - part[3][1], part[0][0] - part[1][1])
        imag = jnp.where(held, 0.0, part[1][0] + part[0][1])
        freq_y = jnp.where(half == 0, d, jnp.where(d == 0, ACROSS // 2, ACROSS - d))
        turn = lax.rem(freq_y * (off_y + ACROSS), ACROSS)
        cos_y, sin_y = circle[0, turn], circle[1, turn]
        cos_x = shift[2 * half, pl.ds(off_x + MAX_OFF, 1), :]
        sin_x = shift[2 * half + 1, pl.ds(off_x + MAX_OFF, 1), :]
        cos = cos_x * cos_y - sin_x * sin_y
        sin = sin_x * cos_y + cos_x * sin_y
        turned = jnp.concatenate([real * cos - imag * sin, real * sin + imag * cos], axis=1)
        other = jnp.sum(jnp.where(held, part[4][0] + part[5][1], 0.0), axis=1, keepdims=True)
        even = (lax.rem(small_lane + off_x + 6, 2) == 0) | (half == 1)
        sign = jnp.where(even, 1.0, -1.0) * (cos_y * (2.0 / VOXELS))
        return turned, other * jnp.where(small_lane < WIN, sign, 0.0)

    terms, extra = ([], []), ([], [])
    for first, second, slot in ((0, 1, c), (4, 2, 3 + 2 * c), (5, 3, 4 + 2 * c)):
        real, imag = phase_of(spectrum(first, held), spectrum(second, held), edge)
        for half in range(2):
            rows = slice(DEPTH * half, DEPTH * (half + 1))
            turned, more = window_rows((real[rows], imag[rows]), half, slot)
            terms[half].append(turned)
            extra[half].append(more)
    real, imag = spectrum(6, special(c))
    seam_edge = edges(DEPTH, lambda row: c)
    phase = phase_of((real[:DEPTH], imag[:DEPTH]), (real[DEPTH:], imag[DEPTH:]), seam_edge)
    turned, more = window_rows(phase, c, 2)
    for half in range(2):
        terms[half].append(jnp.where(c == half, turned, 0.0))
        extra[half].append(jnp.where(c == half, more, 0.0))
    sums = []
    for half in range(2):
        high, low = split(jnp.concatenate(terms[half], axis=0))
        table_hi, table_lo = steps[half, 0], steps[half, 1]
        total = dot(high, table_hi) + dot(low, table_hi) + dot(high, table_lo)
        sums.append(total + jnp.concatenate(extra[half], axis=0))
    lane = lax.broadcasted_iota(jnp.int32, sums[0].shape, 1)
    both = sums[0] + jnp.where(lane < 64, sums[1], -sums[1])
    apart = jnp.where(lane < 64, sums[0], pltpu.roll(sums[1], 64, 1))
    both = jnp.where(d == 0, apart, both)
    rows = jnp.concatenate([both[16 * k : 16 * k + WIN] for k in range(4)], axis=0)
    packed = rows[:GROUP]
    for group in range(1, GROUP):
        packed = packed + pltpu.roll(rows[GROUP * group : GROUP * (group + 1)], WIN * group, 1)
    packed = jnp.concatenate([packed, jnp.zeros((2, 128), F32)], axis=0)
    out[...] = jnp.broadcast_to(packed[None], out.shape)


def energy_kernel(where, got, offsets, turns, places, windows, terms):
    sums = [[None] * WIN, [None] * WIN]
    for sub in range(SUBS):
        turn = turns[sub]
        for core in range(2):
            value = got[SUBS * core + sub]
            for step in range(WIN):
                term = value * turn[step : step + 1]
                sums[core][step] = term if sub == 0 else sums[core][step] + term
    sums = [[value + pltpu.roll(value, 64, 1) for value in side] for side in sums]
    seam = [left + right for left, right in zip(*sums)]
    totals = []
    for side in (sums[0], sums[1], seam):
        squares = [value * value for value in side]
        total = squares[0]
        for value in squares[1:]:
            total = total + value
        across = squares[0] * float(-REACH)
        for step in range(1, WIN):
            across = across + squares[step] * float(step - REACH)
        totals.append((total, across))
    slots = ((0, 0), (1, 0), (2, 3), (0, 1), (0, 2), (1, 1), (1, 2))

    def stacked(kind, which):
        rows = [
            jnp.sum(totals[side][which] * places[kind, pair], axis=0, keepdims=True)
            for side, pair in slots
        ]
        rows = jnp.concatenate(rows + [jnp.zeros((1, 128), F32)], axis=0)
        return jnp.sum(rows, axis=1, keepdims=True)

    energy = stacked(0, 0)
    moments = [stacked(1, 0), stacked(0, 1), stacked(2, 0)]
    lane = lax.broadcasted_iota(jnp.int32, (8, 128), 1)
    mixed = jnp.where(lane == 1, moments[0], jnp.where(lane == 2, moments[1], moments[2]))
    place = offsets[...] + mixed / (energy + EPSILON)
    value = jnp.where(lane == 0, energy, energy * place)
    value = jnp.where(lane < 4, value, 0.0)
    terms[...] = jnp.broadcast_to(value[None], terms.shape)
    is_left = where[1] == 0
    at_seam = places[0, 3] > 0.0
    for step in range(WIN):
        mine = jnp.where(is_left, sums[0][step], sums[1][step])
        windows[step] = jnp.where(at_seam, seam[step], mine)


def unpack(packed):
    lane = lax.broadcasted_iota(jnp.int32, (8, 128), 1)
    values = [packed[step] for step in range(WIN)]
    groups = []
    for group in range(GROUP):
        inside = (lane >= WIN * group) & (lane < WIN * (group + 1))
        rows = jnp.zeros((8, 128), F32)
        for step in range(WIN):
            moved = WIN * (step - group) % 128
            value = jnp.where(inside, values[step], 0.0)
            rows = rows + (pltpu.roll(value, moved, 1) if moved else value)
        groups.append(rows[:GROUP])
    rows = jnp.concatenate(groups, axis=0)
    return [rows[WIN * pair : WIN * (pair + 1)] for pair in range(4)]


def graph_kernel(terms, graph, ignored, matrix, rhs):
    del ignored
    table = graph[...]
    value = terms[...].reshape(PLANES * 8, 128)
    weighted = table * value[:, :1]
    over = (((0,), (0,)), ((), ()))
    matrix[...] = lax.dot_general(
        table, weighted, over, precision=lax.Precision.HIGHEST, preferred_element_type=F32
    )
    load = lax.dot_general(
        value, table, over, precision=lax.Precision.HIGHEST, preferred_element_type=F32
    )
    rhs[...] = load[1:4]


def place_kernel(where, meta, mine, below, windows, done):
    done[...] = mine[0]
    c = where[1]
    slot = lax.broadcasted_iota(jnp.int32, (6, 128), 0)
    blocks = unpack(mine) + unpack(below)[1:3]
    places = [slot == meta[k, 3] for k in (c, 3 + 2 * c, 4 + 2 * c, 2, 7, 8)]
    for step in range(WIN):
        rows = jnp.zeros((6, 128), F32)
        for block, place in zip(blocks, places):
            rows = jnp.where(place, block[step : step + 1], rows)
        windows[:, WIN * WIN * step : WIN * WIN * (step + 1)] = rows[:, : WIN * WIN]


def call(kernel, shapes, operands, spaces, **params):
    specs = [pl.BlockSpec(memory_space=space) for space in spaces]
    outs = jax.tree.map(lambda _: pl.BlockSpec(memory_space=pltpu.VMEM), shapes)
    return pl.pallas_call(
        kernel,
        out_shape=shapes,
        in_specs=specs,
        out_specs=outs,
        compiler_params=pltpu.CompilerParams(vmem_limit_bytes=16 * 1024 * 1024),
        **params,
    )(*operands)


def local(strips, pair_tiles, pair_owner, pair_offset):
    where = jnp.stack([lax.axis_index(name) for name in ("z", "core", "sub")]).astype(jnp.int32)
    tables = plane_dft_tables()
    depth = lane_tiles(np.concatenate(split_np(depth_table()), axis=0))
    vhi, vlo = split_np(window_table())
    vmem, smem = pltpu.VMEM, pltpu.SMEM

    tiles = strips.reshape(8, LOCAL * ACROSS, ALONG)
    bottoms = jnp.stack([tiles[3], tiles[7]])
    from_above = lax.ppermute(bottoms, "z", [(k, k + 1) for k in range(PLANES - 1)])
    core, bottoms = lax.optimization_barrier((where[1], bottoms))
    own = lax.dynamic_index_in_dim(tiles, 5 - 5 * core, 0, keepdims=False)
    other = lax.ppermute(own, "core", [(0, 1), (1, 0)])

    here = call(
        local_kernel, jax.ShapeDtypeStruct((SUBS, 64, 2 * HALF), BF), (tiles, tables), (vmem, vmem)
    )
    sent, facts, offsets = call(
        remote_kernel,
        (
            jax.ShapeDtypeStruct((SUBS, 112, 2 * HALF), BF),
            jax.ShapeDtypeStruct((16, 128), jnp.int32),
            jax.ShapeDtypeStruct((8, 128), F32),
        ),
        (
            where, here, from_above, own, other, tables,
            pair_tiles.T, pair_owner.reshape(1, -1), pair_offset.T,
        ),
        (smem,) + (vmem,) * 8,
        scratch_shapes=[pltpu.SemaphoreType.DMA],
    )
    got = lax.all_to_all(sent, "sub", split_axis=0, concat_axis=0, tiled=True)
    partial = call(
        window_kernel,
        jax.ShapeDtypeStruct((2 * SUBS, 8, 128), F32),
        (where, facts, circle_table(), got, depth, vhi, vlo, step_table(), shift_table()),
        (smem,) * 3 + (vmem,) * 6,
    )
    shares = lax.all_to_all(partial, ("core", "sub"), split_axis=0, concat_axis=0, tiled=True)
    mine, terms = call(
        energy_kernel,
        (jax.ShapeDtypeStruct((WIN, 8, 128), F32), jax.ShapeDtypeStruct((PLANES, 8, 128), F32)),
        (where, shares, offsets, turn_table(), place_table()),
        (smem, vmem, vmem, vmem, vmem),
    )
    below = lax.ppermute(mine, "z", [(k + 1, k) for k in range(PLANES - 1)])
    all_terms = lax.all_to_all(terms, "z", split_axis=0, concat_axis=0, tiled=True)
    windows, done = call(
        place_kernel,
        (jax.ShapeDtypeStruct((6, WIN * WIN * WIN), F32), jax.ShapeDtypeStruct((8, 128), F32)),
        (where, facts, mine, below),
        (smem, smem, vmem, vmem),
    )
    matrix, rhs = call(
        graph_kernel,
        (jax.ShapeDtypeStruct((64, 64), F32), jax.ShapeDtypeStruct((3, 64), F32)),
        (all_terms, graph_table(), done),
        (vmem, vmem, pl.ANY),
    )
    return windows, matrix, rhs.T


def solution(mesh):
    grid = Mesh(mesh.devices.reshape(PLANES, 2, SUBS), ("z", "core", "sub"))
    tiles = ("z", "core")
    in_specs = (P(tiles, None, "sub", None, None), P(), P(), P())
    out_specs = (P(tiles, None), P(), P())
    return jax.shard_map(local, mesh=grid, in_specs=in_specs, out_specs=out_specs, check_vma=False)
```

```python
import jax
import jax.numpy as jnp
import ml_dtypes
import numpy as np
from jax import lax
from jax.experimental import pallas as pl
from jax.experimental.pallas import tpu as pltpu
from jax.sharding import Mesh, PartitionSpec as P

REACH = 4
WIN = 9
EPSILON = 1e-06
FLOOR_SHARE = 0.05
ROW = 4
PLANES = 16
SUBS = 16
DEPTH, ACROSS, ALONG = 128, 32, 256
LOCAL = DEPTH // SUBS
HALF = ALONG // 2
VOXELS = DEPTH * ACROSS * ALONG
MAX_OFF = 5
OFFS = 2 * MAX_OFF + 1
BF = jnp.bfloat16
F32 = jnp.float32


def split_np(table):
    high = table.astype(ml_dtypes.bfloat16)
    low = (table - high.astype(np.float64)).astype(ml_dtypes.bfloat16)
    return high, low


def lane_tiles(table):
    return np.stack([table[..., :128], table[..., 128:]], axis=-3)


def angles(rows, cols, length):
    return (np.outer(rows, cols) % length) * (2.0 * np.pi / length)


def across_freq(half, sub):
    if half == 0:
        return sub
    return ACROSS // 2 if sub == 0 else ACROSS - sub


def across_table():
    table = np.zeros((2, 2, SUBS, LOCAL, LOCAL, ACROSS))
    for half in range(2):
        for sub in range(SUBS):
            theta = angles([across_freq(half, sub)], np.arange(ACROSS), ACROSS)[0]
            for plane in range(LOCAL):
                table[half, 0, sub, plane, plane] = np.cos(theta)
                table[half, 1, sub, plane, plane] = -np.sin(theta)
    return table.reshape(2, 2 * SUBS * LOCAL, LOCAL * ACROSS)


def along_table():
    table = np.zeros((2, 2, ALONG, 2, HALF))
    for half in range(2):
        theta = angles(np.arange(ALONG), np.arange(HALF) + half, ALONG)
        table[half, 0, :, 0] = np.cos(theta)
        table[half, 0, :, 1] = -np.sin(theta)
        table[half, 1, :, 0] = np.sin(theta)
        table[half, 1, :, 1] = np.cos(theta)
    return table.reshape(2, 2 * ALONG, 2 * HALF)


def extra_table():
    table = np.zeros((2, ALONG, HALF))
    table[0, :, 0] = np.where(np.arange(ALONG) % 2 == 0, 1.0, -1.0)
    table[1, :, HALF - 1] = 1.0
    return table


HALF_ROWS = 2 * SUBS * LOCAL


def plane_dft_tables():
    across, along = split_np(across_table()), split_np(along_table())
    extra = extra_table().astype(ml_dtypes.bfloat16)
    pieces = [part[half] for half in range(2) for part in across]
    pieces += [part[half] for half in range(2) for part in along]
    pieces.append(np.concatenate([extra[0], extra[1]], axis=1))
    return lane_tiles(np.concatenate(pieces, axis=0))


def wide_rows(tables, start, count):
    rows = pl.ds(pl.multiple_of(start, 256), count)
    return jnp.concatenate([tables[0, rows, :], tables[1, rows, :]], axis=1)


def across_rows(tables, half, low):
    return wide_rows(tables, (2 * half + low) * HALF_ROWS, HALF_ROWS)


def along_rows(tables, half, low):
    start = 4 * HALF_ROWS + (2 * half + low) * 2 * ALONG
    return wide_rows(tables, start, 2 * ALONG)


def extra_rows(tables, half):
    start = 4 * HALF_ROWS + 8 * ALONG
    return tables[half, start : start + ALONG, :]


def depth_table():
    theta = angles(np.arange(64), np.arange(DEPTH), DEPTH)
    cos, sin = np.cos(theta), np.sin(theta)
    sin[0] = np.where(np.arange(DEPTH) % 2 == 0, 1.0, -1.0)
    table = np.zeros((2, 2, 64, SUBS, 2, LOCAL))
    for half in range(2):
        table[0, half, :, :, half, :] = cos.reshape(64, SUBS, LOCAL)
        table[1, half, :, :, half, :] = sin.reshape(64, SUBS, LOCAL)
    return table.reshape(4 * 64, 2 * DEPTH)


ORDER = np.concatenate([np.arange(65), np.arange(127, 64, -1)])


def window_table():
    freq = np.arange(DEPTH)
    table = np.zeros((OFFS, 6, 16, DEPTH))
    low, high = (freq >= 1) & (freq < 64), freq > 64
    for index in range(OFFS):
        steps = np.arange(WIN) - REACH + index - MAX_OFF
        theta = angles(steps, freq, DEPTH)
        cos, sin = np.cos(theta), np.sin(theta)
        edge = 0.5 * cos * ((freq == 0) | (freq == 64))
        table[index, 0, :WIN] = cos
        table[index, 1, :WIN] = sin
        table[index, 2, :WIN] = cos * low + edge
        table[index, 3, :WIN] = sin * low
        table[index, 4, :WIN] = cos * high
        table[index, 5, :WIN] = edge - sin * high
    return table.reshape(OFFS, 96, DEPTH)[:, :, ORDER]


def step_table():
    step = np.arange(WIN) - REACH
    table = np.zeros((2, 2, HALF, 128))
    for half in range(2):
        theta = angles(np.arange(HALF) + half, step, ALONG)
        table[half, 0, :, :WIN] = np.cos(theta)
        table[half, 1, :, :WIN] = -np.sin(theta)
        table[half, 0, :, 64 : 64 + WIN] = np.sin(theta)
        table[half, 1, :, 64 : 64 + WIN] = np.cos(theta)
    high, low = split_np(table.reshape(2, 2 * HALF, 128) * (2.0 / VOXELS))
    return np.stack([high, low], axis=1)


def turn_table():
    step = np.arange(WIN) - REACH
    table = np.zeros((SUBS, 16, 128), np.float32)
    for sub in range(SUBS):
        theta = angles(step, [sub], ACROSS)
        table[sub, :WIN, :64] = np.cos(theta)
        table[sub, :WIN, 64:] = -np.sin(theta)
    table[0, :WIN, 64:] = np.where(step % 2 == 0, 1.0, -1.0)[:, None]
    return table


def shift_table():
    table = np.zeros((2, 2, 16, HALF))
    for half in range(2):
        theta = angles(np.arange(OFFS) - MAX_OFF, np.arange(HALF) + half, ALONG)
        table[half, 0, :OFFS] = np.cos(theta)
        table[half, 1, :OFFS] = np.sin(theta)
    return table.reshape(4, 16, HALF).astype(np.float32)


GROUP = 6


def place_table():
    table = np.zeros((3, 4, 8, 128), np.float32)
    for index in range(4 * WIN):
        pair, depth = divmod(index, WIN)
        group, row = divmod(index, GROUP)
        for along in range(WIN):
            table[:, pair, row, WIN * group + along] = (1.0, depth - REACH, along - REACH)
    return table


def circle_table():
    theta = np.arange(ACROSS) * (2.0 * np.pi / ACROSS)
    return np.stack([np.cos(theta), np.sin(theta)]).astype(np.float32)


def graph_table():
    table = np.zeros((8, PLANES, ROW * PLANES), np.float32)
    for plane in range(PLANES):
        base = ROW * plane
        pairs = [(base, base + 1), (base + 2, base + 3), (base + 1, base + 2)]
        pairs += [(base - ROW + col, base + col) for col in range(ROW)]
        for slot, (first, second) in enumerate(pairs):
            if first >= 0:
                table[slot, plane, first] = 1.0
                table[slot, plane, second] = -1.0
    return table.reshape(PLANES * 8, ROW * PLANES)


def dot(left, right):
    return jnp.dot(left, right, preferred_element_type=F32)


def split(value):
    high = value.astype(BF)
    return high, (value - high.astype(F32)).astype(BF)


def across_dft(strip, half, tables):
    both = dot(across_rows(tables, half, 0), strip) + dot(across_rows(tables, half, 1), strip)
    rows = SUBS * LOCAL
    return jnp.concatenate([both[:rows], both[rows:]], axis=1)


def along_dft(value, half, tables, count):
    high, low = split(value)
    table_hi, table_lo = along_rows(tables, half, 0), along_rows(tables, half, 1)
    out = dot(high, table_hi) + dot(low, table_hi) + dot(high, table_lo)
    extra = extra_rows(tables, half)
    rows = SUBS * LOCAL
    edge_hi = jnp.concatenate([high[rows * k : rows * k + 16, :ALONG] for k in range(count)], axis=0)
    edge_lo = jnp.concatenate([low[rows * k : rows * k + 16, :ALONG] for k in range(count)], axis=0)
    more = dot(edge_hi, extra) + dot(edge_lo, extra)
    pieces = []
    for k in range(count):
        block = out[rows * k : rows * (k + 1)]
        head = block[:LOCAL]
        head = jnp.concatenate(
            [head[:, :HALF], head[:, HALF:] + more[16 * k : 16 * k + LOCAL]], axis=1
        )
        pieces.append(jnp.concatenate([head, block[LOCAL:]], axis=0).reshape(SUBS, LOCAL, 2 * HALF))
    return pieces


def pair_facts(where, pair_tiles, owner, pair_offset):
    plane, core = where[0], where[1]
    base = ROW * plane
    count = owner.shape[1]
    row = lax.broadcasted_iota(jnp.int32, (16, count), 0)
    place = lax.broadcasted_iota(jnp.int32, (16, count), 1)
    home = 2 * base + jnp.where(row == 1, 4, jnp.where(row == 2, 2, 0))
    up = 2 * (base - ROW + row - 3) + 1
    down = 2 * (base + 2 * core + row - 7) + 1
    wanted = jnp.where(row < 3, home, jnp.where(row < 7, up, jnp.where(row < 9, down, -100)))
    first, second = pair_tiles[0:1, :], pair_tiles[1:2, :]
    key = first * 2 + jnp.where(second - first == 1, 0, 1)
    match = wanted == key
    owned = jnp.broadcast_to(owner[...] == 2 * plane + core, match.shape)

    def total(mask, value):
        return jnp.sum(jnp.where(mask, value, 0), axis=1, keepdims=True)

    offset = [total(match, jnp.broadcast_to(pair_offset[k : k + 1, :], match.shape)) for k in range(3)]
    at = total(match, place)
    held = total(match & owned, 1)
    ordinal = total((place < at) & owned, 1)
    return offset, jnp.where(held > 0, ordinal, -1)


def chunk(pieces):
    return jnp.concatenate(pieces, axis=1).astype(BF)


def local_kernel(strips, tables, out):
    chosen = (1, 4, 2, 6)
    parts = []
    for half in range(2):
        stack = [across_dft(strips[k], half, tables) for k in chosen]
        parts.append(along_dft(jnp.concatenate(stack, axis=0), half, tables, 4))
    for k in range(4):
        out[:, 16 * k : 16 * k + 16, :] = chunk([parts[0][k], parts[1][k]])


def remote_kernel(
    where, here, below, own, other, tables, pair_tiles, owner, pair_offset,
    out, facts, offsets, moved,
):
    kept = pltpu.make_async_copy(here, out.at[:, pl.ds(0, 64), :], moved)
    kept.start()
    offset, slot = pair_facts(where, pair_tiles, owner, pair_offset)
    lane = lax.broadcasted_iota(jnp.int32, (16, 128), 1)
    facts[...] = jnp.where(
        lane == 0, offset[0], jnp.where(lane == 1, offset[1], jnp.where(lane == 2, offset[2], slot))
    )
    lane = lane[:8]
    offsets[...] = jnp.where(
        lane == 1, offset[0][:8], jnp.where(lane == 2, offset[1][:8], offset[2][:8])
    ).astype(F32)
    parts = []
    for half in range(2):
        stack = [across_dft(below[k], half, tables) for k in range(2)]
        parts.append(along_dft(jnp.concatenate(stack, axis=0), half, tables, 2))
    for k in range(2):
        out[:, 64 + 16 * k : 80 + 16 * k, :] = chunk([parts[0][k], parts[1][k]])
    core = where[1]
    mine, theirs = own[...], other[...]
    first = jnp.where(core == 0, mine, theirs)
    second = jnp.where(core == 0, theirs, mine)
    stack = [across_dft(strip, core, tables) for strip in (first, second)]
    out[:, 96:112, :] = chunk(along_dft(jnp.concatenate(stack, axis=0), core, tables, 2))
    kept.wait()


def spectrum_of(block, zeroth, held, depth_hi, depth_lo):
    both = dot(depth_hi, block) + dot(depth_lo, block)
    cos, sin = both[:DEPTH], both[DEPTH:]
    cos_re, cos_im = cos[:, :HALF], cos[:, HALF:]
    sin_re, sin_im = sin[:, :HALF], sin[:, HALF:]
    low_re = jnp.where(zeroth | held, cos_re, cos_re + sin_im)
    low_im = jnp.where(zeroth, cos_im, jnp.where(held, 0.0, cos_im) - sin_re)
    high_re = jnp.where(zeroth, sin_re, jnp.where(held, cos_im, cos_re - sin_im))
    high_im = jnp.where(zeroth, sin_im, jnp.where(held, sin_im, cos_im + sin_re))

    def rows(low, high):
        return jnp.concatenate([low[:64], high[:64], low[64:], high[64:]], axis=0)

    return rows(low_re, high_re), rows(low_im, high_im)


def phase_of(first, second, edge):
    floor = (FLOOR_SHARE * VOXELS) ** 2
    first_re, first_im = first
    second_re, second_im = second
    straight, crossed = first_re * second_re, first_im * second_im
    imag = first_im * second_re - first_re * second_im
    if edge is None:
        real = straight + crossed
        norm = lax.rsqrt(real * real + imag * imag + floor)
        return real * norm, imag * norm
    real = straight + jnp.where(edge, 0.0, crossed)
    imag = jnp.where(edge, crossed, imag)
    real_sq, imag_sq = real * real, imag * imag
    norm = lax.rsqrt(real_sq + jnp.where(edge, 0.0, imag_sq) + floor)
    norm_im = jnp.where(edge, lax.rsqrt(imag_sq + floor), norm)
    return real * norm, imag * norm_im


def window_kernel(where, meta, circle, got, depth, vhi, vlo, steps, shift, out):
    c, d = where[1], where[2]
    row = lax.broadcasted_iota(jnp.int32, (DEPTH, HALF), 0)
    lane = lax.broadcasted_iota(jnp.int32, (DEPTH, HALF), 1)
    zeroth = lax.rem(row, 64) == 0
    nowhere = jnp.where(d == 0, 0, 2 * HALF)

    def special(half_of_row):
        return (lane == half_of_row * (HALF - 1) + nowhere) & (lax.rem(row, 64) != 0)

    def edges(count, half_of_row):
        row = lax.broadcasted_iota(jnp.int32, (count, HALF), 0)
        lane = lax.broadcasted_iota(jnp.int32, (count, HALF), 1)
        return (lane == half_of_row(row) * (HALF - 1) + nowhere) & (lax.rem(row, 64) == 0)

    held = special(row // 64)
    edge = edges(2 * DEPTH, lambda row: row // DEPTH)
    depth_hi, depth_lo = wide_rows(depth, 0, 256), wide_rows(depth, 256, 256)

    def spectrum(slot, held):
        block = got[:, 16 * slot : 16 * slot + 16, :].reshape(2 * DEPTH, 2 * HALF)
        return spectrum_of(block, zeroth, held, depth_hi, depth_lo)

    small_lane = lax.broadcasted_iota(jnp.int32, (16, HALF), 1)

    def window_rows(phase, half, slot):
        off_z, off_y, off_x = meta[slot, 0], meta[slot, 1], meta[slot, 2]
        high, low = split(jnp.concatenate(phase, axis=1))
        table_hi, table_lo = vhi[off_z + MAX_OFF], vlo[off_z + MAX_OFF]
        rows = dot(table_hi, high) + dot(table_lo, high) + dot(table_hi, low)
        part = [(rows[16 * k : 16 * k + 16, :HALF], rows[16 * k : 16 * k + 16, HALF:]) for k in range(6)]
        held = small_lane == half * (HALF - 1) + nowhere
        real = jnp.where(held, part[2][0] - part[3][1], part[0][0] - part[1][1])
        imag = jnp.where(held, 0.0, part[1][0] + part[0][1])
        freq_y = jnp.where(half == 0, d, jnp.where(d == 0, ACROSS // 2, ACROSS - d))
        turn = lax.rem(freq_y * (off_y + ACROSS), ACROSS)
        cos_y, sin_y = circle[0, turn], circle[1, turn]
        cos_x = shift[2 * half, pl.ds(off_x + MAX_OFF, 1), :]
        sin_x = shift[2 * half + 1, pl.ds(off_x + MAX_OFF, 1), :]
        cos = cos_x * cos_y - sin_x * sin_y
        sin = sin_x * cos_y + cos_x * sin_y
        turned = jnp.concatenate([real * cos - imag * sin, real * sin + imag * cos], axis=1)
        other = jnp.sum(jnp.where(held, part[4][0] + part[5][1], 0.0), axis=1, keepdims=True)
        even = (lax.rem(small_lane + off_x + 6, 2) == 0) | (half == 1)
        sign = jnp.where(even, 1.0, -1.0) * (cos_y * (2.0 / VOXELS))
        return turned, other * jnp.where(small_lane < WIN, sign, 0.0)

    terms, extra = ([], []), ([], [])
    for first, second, slot in ((0, 1, c), (4, 2, 3 + 2 * c), (5, 3, 4 + 2 * c)):
        real, imag = phase_of(spectrum(first, held), spectrum(second, held), edge)
        for half in range(2):
            rows = slice(DEPTH * half, DEPTH * (half + 1))
            turned, more = window_rows((real[rows], imag[rows]), half, slot)
            terms[half].append(turned)
            extra[half].append(more)
    real, imag = spectrum(6, special(c))
    seam_edge = edges(DEPTH, lambda row: c)
    phase = phase_of((real[:DEPTH], imag[:DEPTH]), (real[DEPTH:], imag[DEPTH:]), seam_edge)
    turned, more = window_rows(phase, c, 2)
    for half in range(2):
        terms[half].append(jnp.where(c == half, turned, 0.0))
        extra[half].append(jnp.where(c == half, more, 0.0))
    sums = []
    for half in range(2):
        high, low = split(jnp.concatenate(terms[half], axis=0))
        table_hi, table_lo = steps[half, 0], steps[half, 1]
        total = dot(high, table_hi) + dot(low, table_hi) + dot(high, table_lo)
        sums.append(total + jnp.concatenate(extra[half], axis=0))
    lane = lax.broadcasted_iota(jnp.int32, sums[0].shape, 1)
    both = sums[0] + jnp.where(lane < 64, sums[1], -sums[1])
    apart = jnp.where(lane < 64, sums[0], pltpu.roll(sums[1], 64, 1))
    both = jnp.where(d == 0, apart, both)
    rows = jnp.concatenate([both[16 * k : 16 * k + WIN] for k in range(4)], axis=0)
    packed = rows[:GROUP]
    for group in range(1, GROUP):
        packed = packed + pltpu.roll(rows[GROUP * group : GROUP * (group + 1)], WIN * group, 1)
    packed = jnp.concatenate([packed, jnp.zeros((2, 128), F32)], axis=0)
    out[...] = jnp.broadcast_to(packed[None], out.shape)


def across_sums(got, turns):
    sums = [[None] * WIN, [None] * WIN]
    for sub in range(SUBS):
        turn = turns[sub]
        for core in range(2):
            value = got[SUBS * core + sub]
            for step in range(WIN):
                term = value * turn[step : step + 1]
                sums[core][step] = term if sub == 0 else sums[core][step] + term
    sums = [[value + pltpu.roll(value, 64, 1) for value in side] for side in sums]
    return sums, [left + right for left, right in zip(*sums)]


def energy_kernel(got, offsets, turns, places, terms):
    sums, seam = across_sums(got, turns)
    totals = []
    for side in (sums[0], sums[1], seam):
        squares = [value * value for value in side]
        total = squares[0]
        for value in squares[1:]:
            total = total + value
        across = squares[0] * float(-REACH)
        for step in range(1, WIN):
            across = across + squares[step] * float(step - REACH)
        totals.append((total, across))
    slots = ((0, 0), (1, 0), (2, 3), (0, 1), (0, 2), (1, 1), (1, 2))

    def stacked(kind, which):
        rows = [
            jnp.sum(totals[side][which] * places[kind, pair], axis=0, keepdims=True)
            for side, pair in slots
        ]
        rows = jnp.concatenate(rows + [jnp.zeros((1, 128), F32)], axis=0)
        return jnp.sum(rows, axis=1, keepdims=True)

    energy = stacked(0, 0)
    moments = [stacked(1, 0), stacked(0, 1), stacked(2, 0)]
    lane = lax.broadcasted_iota(jnp.int32, (8, 128), 1)
    mixed = jnp.where(lane == 1, moments[0], jnp.where(lane == 2, moments[1], moments[2]))
    place = offsets[...] + mixed / (energy + EPSILON)
    value = jnp.where(lane == 0, energy, energy * place)
    value = jnp.where(lane < 4, value, 0.0)
    line = value[0:1]
    for slot in range(1, 7):
        line = line + pltpu.roll(value[slot : slot + 1], 4 * slot, 1)
    terms[...] = jnp.broadcast_to(line[None], terms.shape)


def values_kernel(where, got, turns, places, ignored, windows):
    del ignored
    sums, seam = across_sums(got, turns)
    is_left = where[1] == 0
    at_seam = places[0, 3] > 0.0
    for step in range(WIN):
        mine = jnp.where(is_left, sums[0][step], sums[1][step])
        windows[step] = jnp.where(at_seam, seam[step], mine)


def unpack(packed):
    lane = lax.broadcasted_iota(jnp.int32, (8, 128), 1)
    values = [packed[step] for step in range(WIN)]
    groups = []
    for group in range(GROUP):
        inside = (lane >= WIN * group) & (lane < WIN * (group + 1))
        rows = jnp.zeros((8, 128), F32)
        for step in range(WIN):
            moved = WIN * (step - group) % 128
            value = jnp.where(inside, values[step], 0.0)
            rows = rows + (pltpu.roll(value, moved, 1) if moved else value)
        groups.append(rows[:GROUP])
    rows = jnp.concatenate(groups, axis=0)
    return [rows[WIN * pair : WIN * (pair + 1)] for pair in range(4)]


def graph_kernel(terms, graph, turned, ignored, matrix, rhs):
    del ignored
    lines = jnp.concatenate([terms[plane, 0:1] for plane in range(PLANES)], axis=0)
    slots = [lines] + [pltpu.roll(lines, 128 - 4 * slot, 1) for slot in range(1, 8)]
    value = jnp.concatenate(slots, axis=0)
    wide = jnp.concatenate([graph[...] * value[:, :1], value[:, :64]], axis=1)
    high, rest = wide.astype(BF), wide - wide.astype(BF).astype(F32)
    middle, low = split(rest)
    table = turned[...]
    both = dot(table, high) + dot(table, middle) + dot(table, low)
    matrix[...] = both[:, :64]
    rhs[...] = both.T[65:68]


def place_kernel(where, meta, mine, below, windows, done):
    done[...] = mine[0]
    c = where[1]
    slot = lax.broadcasted_iota(jnp.int32, (6, 128), 0)
    blocks = unpack(mine) + unpack(below)[1:3]
    places = [slot == meta[k, 3] for k in (c, 3 + 2 * c, 4 + 2 * c, 2, 7, 8)]
    for step in range(WIN):
        rows = jnp.zeros((6, 128), F32)
        for block, place in zip(blocks, places):
            rows = jnp.where(place, block[step : step + 1], rows)
        windows[:, WIN * WIN * step : WIN * WIN * (step + 1)] = rows[:, : WIN * WIN]


def call(kernel, shapes, operands, spaces, **params):
    specs = [pl.BlockSpec(memory_space=space) for space in spaces]
    outs = jax.tree.map(lambda _: pl.BlockSpec(memory_space=pltpu.VMEM), shapes)
    return pl.pallas_call(
        kernel,
        out_shape=shapes,
        in_specs=specs,
        out_specs=outs,
        compiler_params=pltpu.CompilerParams(vmem_limit_bytes=16 * 1024 * 1024),
        **params,
    )(*operands)


def local(strips, pair_tiles, pair_owner, pair_offset):
    where = jnp.stack([lax.axis_index(name) for name in ("z", "core", "sub")]).astype(jnp.int32)
    tables = plane_dft_tables()
    depth = lane_tiles(np.concatenate(split_np(depth_table()), axis=0))
    vhi, vlo = split_np(window_table())
    vmem, smem = pltpu.VMEM, pltpu.SMEM

    tiles = strips.reshape(8, LOCAL * ACROSS, ALONG)
    bottoms = jnp.stack([tiles[3], tiles[7]])
    from_above = lax.ppermute(bottoms, "z", [(k, k + 1) for k in range(PLANES - 1)])
    core, bottoms = lax.optimization_barrier((where[1], bottoms))
    own = lax.dynamic_index_in_dim(tiles, 5 - 5 * core, 0, keepdims=False)
    other = lax.ppermute(own, "core", [(0, 1), (1, 0)])

    here = call(
        local_kernel, jax.ShapeDtypeStruct((SUBS, 64, 2 * HALF), BF), (tiles, tables), (vmem, vmem)
    )
    sent, facts, offsets = call(
        remote_kernel,
        (
            jax.ShapeDtypeStruct((SUBS, 112, 2 * HALF), BF),
            jax.ShapeDtypeStruct((16, 128), jnp.int32),
            jax.ShapeDtypeStruct((8, 128), F32),
        ),
        (
            where, here, from_above, own, other, tables,
            pair_tiles.T, pair_owner.reshape(1, -1), pair_offset.T,
        ),
        (smem,) + (vmem,) * 8,
        scratch_shapes=[pltpu.SemaphoreType.DMA],
    )
    got = lax.all_to_all(sent, "sub", split_axis=0, concat_axis=0, tiled=True)
    partial = call(
        window_kernel,
        jax.ShapeDtypeStruct((2 * SUBS, 8, 128), F32),
        (where, facts, circle_table(), got, depth, vhi, vlo, step_table(), shift_table()),
        (smem,) * 3 + (vmem,) * 6,
    )
    shares = lax.all_to_all(partial, ("core", "sub"), split_axis=0, concat_axis=0, tiled=True)
    terms = call(
        energy_kernel,
        jax.ShapeDtypeStruct((PLANES, 8, 128), F32),
        (shares, offsets, turn_table(), place_table()),
        (vmem,) * 4,
    )
    mine = call(
        values_kernel,
        jax.ShapeDtypeStruct((WIN, 8, 128), F32),
        (where, shares, turn_table(), place_table(), terms),
        (smem, vmem, vmem, vmem, pl.ANY),
    )
    below = lax.ppermute(mine, "z", [(k + 1, k) for k in range(PLANES - 1)])
    all_terms = lax.all_to_all(terms, "z", split_axis=0, concat_axis=0, tiled=True)
    windows, done = call(
        place_kernel,
        (jax.ShapeDtypeStruct((6, WIN * WIN * WIN), F32), jax.ShapeDtypeStruct((8, 128), F32)),
        (where, facts, mine, below),
        (smem, smem, vmem, vmem),
    )
    matrix, rhs = call(
        graph_kernel,
        (jax.ShapeDtypeStruct((64, 64), F32), jax.ShapeDtypeStruct((3, 64), F32)),
        (all_terms, graph_table(), graph_table().T.astype(ml_dtypes.bfloat16), done),
        (vmem, vmem, vmem, pl.ANY),
    )
    return windows, matrix, rhs.T


def solution(mesh):
    grid = Mesh(mesh.devices.reshape(PLANES, 2, SUBS), ("z", "core", "sub"))
    tiles = ("z", "core")
    in_specs = (P(tiles, None, "sub", None, None), P(), P(), P())
    out_specs = (P(tiles, None), P(), P())
    return jax.shard_map(local, mesh=grid, in_specs=in_specs, out_specs=out_specs, check_vma=False)
```

```python
import jax
import jax.numpy as jnp
import ml_dtypes
import numpy as np
from jax import lax
from jax.experimental import pallas as pl
from jax.experimental.pallas import tpu as pltpu
from jax.sharding import Mesh, PartitionSpec as P

REACH = 4
WIN = 9
EPSILON = 1e-06
FLOOR_SHARE = 0.05
ROW = 4
PLANES = 16
SUBS = 16
DEPTH, ACROSS, ALONG = 128, 32, 256
LOCAL = DEPTH // SUBS
HALF = ALONG // 2
VOXELS = DEPTH * ACROSS * ALONG
MAX_OFF = 5
OFFS = 2 * MAX_OFF + 1
BF = jnp.bfloat16
F32 = jnp.float32


def split_np(table):
    high = table.astype(ml_dtypes.bfloat16)
    low = (table - high.astype(np.float64)).astype(ml_dtypes.bfloat16)
    return high, low


def lane_tiles(table):
    return np.stack([table[..., :128], table[..., 128:]], axis=-3)


def angles(rows, cols, length):
    return (np.outer(rows, cols) % length) * (2.0 * np.pi / length)


def across_freq(half, sub):
    if half == 0:
        return sub
    return ACROSS // 2 if sub == 0 else ACROSS - sub


def across_table():
    table = np.zeros((2, 2, SUBS, LOCAL, LOCAL, ACROSS))
    for half in range(2):
        for sub in range(SUBS):
            theta = angles([across_freq(half, sub)], np.arange(ACROSS), ACROSS)[0]
            for plane in range(LOCAL):
                table[half, 0, sub, plane, plane] = np.cos(theta)
                table[half, 1, sub, plane, plane] = -np.sin(theta)
    return table.reshape(2, 2 * SUBS * LOCAL, LOCAL * ACROSS)


def along_table():
    table = np.zeros((2, 2, ALONG, 2, HALF))
    for half in range(2):
        theta = angles(np.arange(ALONG), np.arange(HALF) + half, ALONG)
        table[half, 0, :, 0] = np.cos(theta)
        table[half, 0, :, 1] = -np.sin(theta)
        table[half, 1, :, 0] = np.sin(theta)
        table[half, 1, :, 1] = np.cos(theta)
    return table.reshape(2, 2 * ALONG, 2 * HALF)


def extra_table():
    table = np.zeros((2, ALONG, HALF))
    table[0, :, 0] = np.where(np.arange(ALONG) % 2 == 0, 1.0, -1.0)
    table[1, :, HALF - 1] = 1.0
    return table


HALF_ROWS = 2 * SUBS * LOCAL


def plane_dft_tables():
    across, along = split_np(across_table()), split_np(along_table())
    extra = extra_table().astype(ml_dtypes.bfloat16)
    pieces = [part[half] for half in range(2) for part in across]
    pieces += [part[half] for half in range(2) for part in along]
    pieces.append(np.concatenate([extra[0], extra[1]], axis=1))
    return lane_tiles(np.concatenate(pieces, axis=0))


def wide_rows(tables, start, count):
    rows = pl.ds(pl.multiple_of(start, 256), count)
    return jnp.concatenate([tables[0, rows, :], tables[1, rows, :]], axis=1)


def across_rows(tables, half, low):
    return wide_rows(tables, (2 * half + low) * HALF_ROWS, HALF_ROWS)


def along_rows(tables, half, low):
    start = 4 * HALF_ROWS + (2 * half + low) * 2 * ALONG
    return wide_rows(tables, start, 2 * ALONG)


def extra_rows(tables, half):
    start = 4 * HALF_ROWS + 8 * ALONG
    return tables[half, start : start + ALONG, :]


def depth_table():
    theta = angles(np.arange(64), np.arange(DEPTH), DEPTH)
    cos, sin = np.cos(theta), np.sin(theta)
    sin[0] = np.where(np.arange(DEPTH) % 2 == 0, 1.0, -1.0)
    table = np.zeros((2, 2, 64, SUBS, 2, LOCAL))
    for half in range(2):
        table[0, half, :, :, half, :] = cos.reshape(64, SUBS, LOCAL)
        table[1, half, :, :, half, :] = sin.reshape(64, SUBS, LOCAL)
    return table.reshape(4 * 64, 2 * DEPTH)


ORDER = np.concatenate([np.arange(65), np.arange(127, 64, -1)])


def window_table():
    freq = np.arange(DEPTH)
    table = np.zeros((OFFS, 6, 16, DEPTH))
    low, high = (freq >= 1) & (freq < 64), freq > 64
    for index in range(OFFS):
        steps = np.arange(WIN) - REACH + index - MAX_OFF
        theta = angles(steps, freq, DEPTH)
        cos, sin = np.cos(theta), np.sin(theta)
        edge = 0.5 * cos * ((freq == 0) | (freq == 64))
        table[index, 0, :WIN] = cos
        table[index, 1, :WIN] = sin
        table[index, 2, :WIN] = cos * low + edge
        table[index, 3, :WIN] = sin * low
        table[index, 4, :WIN] = cos * high
        table[index, 5, :WIN] = edge - sin * high
    return table.reshape(OFFS, 96, DEPTH)[:, :, ORDER]


def step_table():
    step = np.arange(WIN) - REACH
    table = np.zeros((2, 2, HALF, 128))
    for half in range(2):
        theta = angles(np.arange(HALF) + half, step, ALONG)
        table[half, 0, :, :WIN] = np.cos(theta)
        table[half, 1, :, :WIN] = -np.sin(theta)
        table[half, 0, :, 64 : 64 + WIN] = np.sin(theta)
        table[half, 1, :, 64 : 64 + WIN] = np.cos(theta)
    high, low = split_np(table.reshape(2, 2 * HALF, 128) * (2.0 / VOXELS))
    return np.stack([high, low], axis=1)


def turn_table():
    step = np.arange(WIN) - REACH
    table = np.zeros((SUBS, 16, 128), np.float32)
    for sub in range(SUBS):
        theta = angles(step, [sub], ACROSS)
        table[sub, :WIN, :64] = np.cos(theta)
        table[sub, :WIN, 64:] = -np.sin(theta)
    table[0, :WIN, 64:] = np.where(step % 2 == 0, 1.0, -1.0)[:, None]
    return table


def shift_table():
    table = np.zeros((2, 2, 16, HALF))
    for half in range(2):
        theta = angles(np.arange(OFFS) - MAX_OFF, np.arange(HALF) + half, ALONG)
        table[half, 0, :OFFS] = np.cos(theta)
        table[half, 1, :OFFS] = np.sin(theta)
    return table.reshape(4, 16, HALF).astype(np.float32)


GROUP = 6


def place_table():
    table = np.zeros((3, 4, 8, 128), np.float32)
    for index in range(4 * WIN):
        pair, depth = divmod(index, WIN)
        group, row = divmod(index, GROUP)
        for along in range(WIN):
            table[:, pair, row, WIN * group + along] = (1.0, depth - REACH, along - REACH)
    return table


def circle_table():
    theta = np.arange(ACROSS) * (2.0 * np.pi / ACROSS)
    return np.stack([np.cos(theta), np.sin(theta)]).astype(np.float32)


def graph_table():
    table = np.zeros((8, PLANES, ROW * PLANES), np.float32)
    for plane in range(PLANES):
        base = ROW * plane
        pairs = [(base, base + 1), (base + 2, base + 3), (base + 1, base + 2)]
        pairs += [(base - ROW + col, base + col) for col in range(ROW)]
        for slot, (first, second) in enumerate(pairs):
            if first >= 0:
                table[slot, plane, first] = 1.0
                table[slot, plane, second] = -1.0
    return table.reshape(PLANES * 8, ROW * PLANES)


def dot(left, right):
    return jnp.dot(left, right, preferred_element_type=F32)


def split(value):
    high = value.astype(BF)
    return high, (value - high.astype(F32)).astype(BF)


def across_dft(strip, half, tables):
    both = dot(across_rows(tables, half, 0), strip) + dot(across_rows(tables, half, 1), strip)
    rows = SUBS * LOCAL
    return jnp.concatenate([both[:rows], both[rows:]], axis=1)


def along_dft(value, half, tables, count):
    high, low = split(value)
    table_hi, table_lo = along_rows(tables, half, 0), along_rows(tables, half, 1)
    out = dot(high, table_hi) + dot(low, table_hi) + dot(high, table_lo)
    extra = extra_rows(tables, half)
    rows = SUBS * LOCAL
    edge_hi = jnp.concatenate([high[rows * k : rows * k + 16, :ALONG] for k in range(count)], axis=0)
    edge_lo = jnp.concatenate([low[rows * k : rows * k + 16, :ALONG] for k in range(count)], axis=0)
    more = dot(edge_hi, extra) + dot(edge_lo, extra)
    pieces = []
    for k in range(count):
        block = out[rows * k : rows * (k + 1)]
        head = block[:LOCAL]
        head = jnp.concatenate(
            [head[:, :HALF], head[:, HALF:] + more[16 * k : 16 * k + LOCAL]], axis=1
        )
        pieces.append(jnp.concatenate([head, block[LOCAL:]], axis=0).reshape(SUBS, LOCAL, 2 * HALF))
    return pieces


def pair_facts(where, pair_tiles, owner, pair_offset):
    plane, core = where[0], where[1]
    base = ROW * plane
    count = owner.shape[1]
    row = lax.broadcasted_iota(jnp.int32, (16, count), 0)
    place = lax.broadcasted_iota(jnp.int32, (16, count), 1)
    home = 2 * base + jnp.where(row == 1, 4, jnp.where(row == 2, 2, 0))
    up = 2 * (base - ROW + row - 3) + 1
    down = 2 * (base + 2 * core + row - 7) + 1
    wanted = jnp.where(row < 3, home, jnp.where(row < 7, up, jnp.where(row < 9, down, -100)))
    first, second = pair_tiles[0:1, :], pair_tiles[1:2, :]
    key = first * 2 + jnp.where(second - first == 1, 0, 1)
    match = wanted == key
    owned = jnp.broadcast_to(owner[...] == 2 * plane + core, match.shape)

    def total(mask, value):
        return jnp.sum(jnp.where(mask, value, 0), axis=1, keepdims=True)

    offset = [total(match, jnp.broadcast_to(pair_offset[k : k + 1, :], match.shape)) for k in range(3)]
    at = total(match, place)
    held = total(match & owned, 1)
    ordinal = total((place < at) & owned, 1)
    return offset, jnp.where(held > 0, ordinal, -1)


def chunk(pieces):
    return jnp.concatenate(pieces, axis=1).astype(BF)


def local_kernel(strips, tables, out):
    chosen = (1, 4, 2, 6)
    parts = []
    for half in range(2):
        stack = [across_dft(strips[k], half, tables) for k in chosen]
        parts.append(along_dft(jnp.concatenate(stack, axis=0), half, tables, 4))
    for k in range(4):
        out[:, 16 * k : 16 * k + 16, :] = chunk([parts[0][k], parts[1][k]])


def seam_kernel(
    where, own, other, tables, pair_tiles, owner, pair_offset, ignored, out, facts, offsets
):
    del ignored
    offset, slot = pair_facts(where, pair_tiles, owner, pair_offset)
    lane = lax.broadcasted_iota(jnp.int32, (16, 128), 1)
    facts[...] = jnp.where(
        lane == 0, offset[0], jnp.where(lane == 1, offset[1], jnp.where(lane == 2, offset[2], slot))
    )
    lane = lane[:8]
    offsets[...] = jnp.where(
        lane == 1, offset[0][:8], jnp.where(lane == 2, offset[1][:8], offset[2][:8])
    ).astype(F32)
    core = where[1]
    mine, theirs = own[...], other[...]
    first = jnp.where(core == 0, mine, theirs)
    second = jnp.where(core == 0, theirs, mine)
    stack = [across_dft(strip, core, tables) for strip in (first, second)]
    out[...] = chunk(along_dft(jnp.concatenate(stack, axis=0), core, tables, 2))


def remote_kernel(here, seam, below, tables, out, moved):
    kept = [
        pltpu.make_async_copy(here, out.at[:, pl.ds(0, 64), :], moved.at[0]),
        pltpu.make_async_copy(seam, out.at[:, pl.ds(96, 16), :], moved.at[1]),
    ]
    for copy in kept:
        copy.start()
    parts = []
    for half in range(2):
        stack = [across_dft(below[k], half, tables) for k in range(2)]
        parts.append(along_dft(jnp.concatenate(stack, axis=0), half, tables, 2))
    for k in range(2):
        out[:, 64 + 16 * k : 80 + 16 * k, :] = chunk([parts[0][k], parts[1][k]])
    for copy in kept:
        copy.wait()


def spectrum_of(block, zeroth, held, depth_hi, depth_lo):
    both = dot(depth_hi, block) + dot(depth_lo, block)
    cos, sin = both[:DEPTH], both[DEPTH:]
    cos_re, cos_im = cos[:, :HALF], cos[:, HALF:]
    sin_re, sin_im = sin[:, :HALF], sin[:, HALF:]
    low_re = jnp.where(zeroth | held, cos_re, cos_re + sin_im)
    low_im = jnp.where(zeroth, cos_im, jnp.where(held, 0.0, cos_im) - sin_re)
    high_re = jnp.where(zeroth, sin_re, jnp.where(held, cos_im, cos_re - sin_im))
    high_im = jnp.where(zeroth, sin_im, jnp.where(held, sin_im, cos_im + sin_re))

    def rows(low, high):
        return jnp.concatenate([low[:64], high[:64], low[64:], high[64:]], axis=0)

    return rows(low_re, high_re), rows(low_im, high_im)


def phase_of(first, second, edge):
    floor = (FLOOR_SHARE * VOXELS) ** 2
    first_re, first_im = first
    second_re, second_im = second
    straight, crossed = first_re * second_re, first_im * second_im
    imag = first_im * second_re - first_re * second_im
    if edge is None:
        real = straight + crossed
        norm = lax.rsqrt(real * real + imag * imag + floor)
        return real * norm, imag * norm
    real = straight + jnp.where(edge, 0.0, crossed)
    imag = jnp.where(edge, crossed, imag)
    real_sq, imag_sq = real * real, imag * imag
    norm = lax.rsqrt(real_sq + jnp.where(edge, 0.0, imag_sq) + floor)
    norm_im = jnp.where(edge, lax.rsqrt(imag_sq + floor), norm)
    return real * norm, imag * norm_im


def window_kernel(where, meta, circle, got, depth, vhi, vlo, steps, shift, out):
    c, d = where[1], where[2]
    row = lax.broadcasted_iota(jnp.int32, (DEPTH, HALF), 0)
    lane = lax.broadcasted_iota(jnp.int32, (DEPTH, HALF), 1)
    zeroth = lax.rem(row, 64) == 0
    nowhere = jnp.where(d == 0, 0, 2 * HALF)

    def special(half_of_row):
        return (lane == half_of_row * (HALF - 1) + nowhere) & (lax.rem(row, 64) != 0)

    def edges(count, half_of_row):
        row = lax.broadcasted_iota(jnp.int32, (count, HALF), 0)
        lane = lax.broadcasted_iota(jnp.int32, (count, HALF), 1)
        return (lane == half_of_row(row) * (HALF - 1) + nowhere) & (lax.rem(row, 64) == 0)

    held = special(row // 64)
    edge = edges(2 * DEPTH, lambda row: row // DEPTH)
    depth_hi, depth_lo = wide_rows(depth, 0, 256), wide_rows(depth, 256, 256)

    def spectrum(slot, held):
        block = got[:, 16 * slot : 16 * slot + 16, :].reshape(2 * DEPTH, 2 * HALF)
        return spectrum_of(block, zeroth, held, depth_hi, depth_lo)

    small_lane = lax.broadcasted_iota(jnp.int32, (16, HALF), 1)

    def window_rows(phase, half, slot):
        off_z, off_y, off_x = meta[slot, 0], meta[slot, 1], meta[slot, 2]
        high, low = split(jnp.concatenate(phase, axis=1))
        table_hi, table_lo = vhi[off_z + MAX_OFF], vlo[off_z + MAX_OFF]
        rows = dot(table_hi, high) + dot(table_lo, high) + dot(table_hi, low)
        part = [(rows[16 * k : 16 * k + 16, :HALF], rows[16 * k : 16 * k + 16, HALF:]) for k in range(6)]
        held = small_lane == half * (HALF - 1) + nowhere
        real = jnp.where(held, part[2][0] - part[3][1], part[0][0] - part[1][1])
        imag = jnp.where(held, 0.0, part[1][0] + part[0][1])
        freq_y = jnp.where(half == 0, d, jnp.where(d == 0, ACROSS // 2, ACROSS - d))
        turn = lax.rem(freq_y * (off_y + ACROSS), ACROSS)
        cos_y, sin_y = circle[0, turn], circle[1, turn]
        cos_x = shift[2 * half, pl.ds(off_x + MAX_OFF, 1), :]
        sin_x = shift[2 * half + 1, pl.ds(off_x + MAX_OFF, 1), :]
        cos = cos_x * cos_y - sin_x * sin_y
        sin = sin_x * cos_y + cos_x * sin_y
        turned = jnp.concatenate([real * cos - imag * sin, real * sin + imag * cos], axis=1)
        other = jnp.sum(jnp.where(held, part[4][0] + part[5][1], 0.0), axis=1, keepdims=True)
        even = (lax.rem(small_lane + off_x + 6, 2) == 0) | (half == 1)
        sign = jnp.where(even, 1.0, -1.0) * (cos_y * (2.0 / VOXELS))
        return turned, other * jnp.where(small_lane < WIN, sign, 0.0)

    terms, extra = ([], []), ([], [])
    for first, second, slot in ((0, 1, c), (4, 2, 3 + 2 * c), (5, 3, 4 + 2 * c)):
        real, imag = phase_of(spectrum(first, held), spectrum(second, held), edge)
        for half in range(2):
            rows = slice(DEPTH * half, DEPTH * (half + 1))
            turned, more = window_rows((real[rows], imag[rows]), half, slot)
            terms[half].append(turned)
            extra[half].append(more)
    real, imag = spectrum(6, special(c))
    seam_edge = edges(DEPTH, lambda row: c)
    phase = phase_of((real[:DEPTH], imag[:DEPTH]), (real[DEPTH:], imag[DEPTH:]), seam_edge)
    turned, more = window_rows(phase, c, 2)
    for half in range(2):
        terms[half].append(jnp.where(c == half, turned, 0.0))
        extra[half].append(jnp.where(c == half, more, 0.0))
    sums = []
    for half in range(2):
        high, low = split(jnp.concatenate(terms[half], axis=0))
        table_hi, table_lo = steps[half, 0], steps[half, 1]
        total = dot(high, table_hi) + dot(low, table_hi) + dot(high, table_lo)
        sums.append(total + jnp.concatenate(extra[half], axis=0))
    lane = lax.broadcasted_iota(jnp.int32, sums[0].shape, 1)
    both = sums[0] + jnp.where(lane < 64, sums[1], -sums[1])
    apart = jnp.where(lane < 64, sums[0], pltpu.roll(sums[1], 64, 1))
    both = jnp.where(d == 0, apart, both)
    rows = jnp.concatenate([both[16 * k : 16 * k + WIN] for k in range(4)], axis=0)
    packed = rows[:GROUP]
    for group in range(1, GROUP):
        packed = packed + pltpu.roll(rows[GROUP * group : GROUP * (group + 1)], WIN * group, 1)
    packed = jnp.concatenate([packed, jnp.zeros((2, 128), F32)], axis=0)
    out[...] = jnp.broadcast_to(packed[None], out.shape)


def across_sums(got, turns):
    sums = [[None] * WIN, [None] * WIN]
    for sub in range(SUBS):
        turn = turns[sub]
        for core in range(2):
            value = got[SUBS * core + sub]
            for step in range(WIN):
                term = value * turn[step : step + 1]
                sums[core][step] = term if sub == 0 else sums[core][step] + term
    sums = [[value + pltpu.roll(value, 64, 1) for value in side] for side in sums]
    return sums, [left + right for left, right in zip(*sums)]


def energy_kernel(got, offsets, turns, places, terms):
    sums, seam = across_sums(got, turns)
    totals = []
    for side in (sums[0], sums[1], seam):
        squares = [value * value for value in side]
        total = squares[0]
        for value in squares[1:]:
            total = total + value
        across = squares[0] * float(-REACH)
        for step in range(1, WIN):
            across = across + squares[step] * float(step - REACH)
        totals.append((total, across))
    slots = ((0, 0), (1, 0), (2, 3), (0, 1), (0, 2), (1, 1), (1, 2))

    def stacked(kind, which):
        rows = [
            jnp.sum(totals[side][which] * places[kind, pair], axis=0, keepdims=True)
            for side, pair in slots
        ]
        rows = jnp.concatenate(rows + [jnp.zeros((1, 128), F32)], axis=0)
        return jnp.sum(rows, axis=1, keepdims=True)

    energy = stacked(0, 0)
    moments = [stacked(1, 0), stacked(0, 1), stacked(2, 0)]
    lane = lax.broadcasted_iota(jnp.int32, (8, 128), 1)
    mixed = jnp.where(lane == 1, moments[0], jnp.where(lane == 2, moments[1], moments[2]))
    place = offsets[...] + mixed / (energy + EPSILON)
    value = jnp.where(lane == 0, energy, energy * place)
    value = jnp.where(lane < 4, value, 0.0)
    line = value[0:1]
    for slot in range(1, 7):
        line = line + pltpu.roll(value[slot : slot + 1], 4 * slot, 1)
    terms[...] = jnp.broadcast_to(line[None], terms.shape)


def values_kernel(where, got, turns, places, ignored, windows):
    del ignored
    sums, seam = across_sums(got, turns)
    is_left = where[1] == 0
    at_seam = places[0, 3] > 0.0
    for step in range(WIN):
        mine = jnp.where(is_left, sums[0][step], sums[1][step])
        windows[step] = jnp.where(at_seam, seam[step], mine)


def unpack(packed):
    lane = lax.broadcasted_iota(jnp.int32, (8, 128), 1)
    values = [packed[step] for step in range(WIN)]
    groups = []
    for group in range(GROUP):
        inside = (lane >= WIN * group) & (lane < WIN * (group + 1))
        rows = jnp.zeros((8, 128), F32)
        for step in range(WIN):
            moved = WIN * (step - group) % 128
            value = jnp.where(inside, values[step], 0.0)
            rows = rows + (pltpu.roll(value, moved, 1) if moved else value)
        groups.append(rows[:GROUP])
    rows = jnp.concatenate(groups, axis=0)
    return [rows[WIN * pair : WIN * (pair + 1)] for pair in range(4)]


def graph_kernel(terms, graph, turned, ignored, matrix, rhs):
    del ignored
    lines = jnp.concatenate([terms[plane, 0:1] for plane in range(PLANES)], axis=0)
    slots = [lines] + [pltpu.roll(lines, 128 - 4 * slot, 1) for slot in range(1, 8)]
    value = jnp.concatenate(slots, axis=0)
    wide = jnp.concatenate([graph[...] * value[:, :1], value[:, :64]], axis=1)
    high, rest = wide.astype(BF), wide - wide.astype(BF).astype(F32)
    middle, low = split(rest)
    table = turned[...]
    both = dot(table, high) + dot(table, middle) + dot(table, low)
    matrix[...] = both[:, :64]
    rhs[...] = both.T[65:68]


def place_kernel(where, meta, mine, below, windows, done):
    done[...] = mine[0]
    c = where[1]
    slot = lax.broadcasted_iota(jnp.int32, (6, 128), 0)
    blocks = unpack(mine) + unpack(below)[1:3]
    places = [slot == meta[k, 3] for k in (c, 3 + 2 * c, 4 + 2 * c, 2, 7, 8)]
    for step in range(WIN):
        rows = jnp.zeros((6, 128), F32)
        for block, place in zip(blocks, places):
            rows = jnp.where(place, block[step : step + 1], rows)
        windows[:, WIN * WIN * step : WIN * WIN * (step + 1)] = rows[:, : WIN * WIN]


def call(kernel, shapes, operands, spaces, **params):
    specs = [pl.BlockSpec(memory_space=space) for space in spaces]
    outs = jax.tree.map(lambda _: pl.BlockSpec(memory_space=pltpu.VMEM), shapes)
    return pl.pallas_call(
        kernel,
        out_shape=shapes,
        in_specs=specs,
        out_specs=outs,
        compiler_params=pltpu.CompilerParams(vmem_limit_bytes=16 * 1024 * 1024),
        **params,
    )(*operands)


def local(strips, pair_tiles, pair_owner, pair_offset):
    where = jnp.stack([lax.axis_index(name) for name in ("z", "core", "sub")]).astype(jnp.int32)
    tables = plane_dft_tables()
    depth = lane_tiles(np.concatenate(split_np(depth_table()), axis=0))
    vhi, vlo = split_np(window_table())
    vmem, smem = pltpu.VMEM, pltpu.SMEM

    tiles = strips.reshape(8, LOCAL * ACROSS, ALONG)
    bottoms = jnp.stack([tiles[3], tiles[7]])
    from_above = lax.ppermute(bottoms, "z", [(k, k + 1) for k in range(PLANES - 1)])
    core, bottoms = lax.optimization_barrier((where[1], bottoms))
    own = lax.dynamic_index_in_dim(tiles, 5 - 5 * core, 0, keepdims=False)
    other = lax.ppermute(own, "core", [(0, 1), (1, 0)])

    here = call(
        local_kernel, jax.ShapeDtypeStruct((SUBS, 64, 2 * HALF), BF), (tiles, tables), (vmem, vmem)
    )
    seam, facts, offsets = call(
        seam_kernel,
        (
            jax.ShapeDtypeStruct((SUBS, 16, 2 * HALF), BF),
            jax.ShapeDtypeStruct((16, 128), jnp.int32),
            jax.ShapeDtypeStruct((8, 128), F32),
        ),
        (
            where, own, other, tables,
            pair_tiles.T, pair_owner.reshape(1, -1), pair_offset.T, here,
        ),
        (smem,) + (vmem,) * 6 + (pl.ANY,),
    )
    sent = call(
        remote_kernel,
        jax.ShapeDtypeStruct((SUBS, 112, 2 * HALF), BF),
        (here, seam, from_above, tables),
        (vmem,) * 4,
        scratch_shapes=[pltpu.SemaphoreType.DMA((2,))],
    )
    got = lax.all_to_all(sent, "sub", split_axis=0, concat_axis=0, tiled=True)
    partial = call(
        window_kernel,
        jax.ShapeDtypeStruct((2 * SUBS, 8, 128), F32),
        (where, facts, circle_table(), got, depth, vhi, vlo, step_table(), shift_table()),
        (smem,) * 3 + (vmem,) * 6,
    )
    shares = lax.all_to_all(partial, ("core", "sub"), split_axis=0, concat_axis=0, tiled=True)
    terms = call(
        energy_kernel,
        jax.ShapeDtypeStruct((PLANES, 8, 128), F32),
        (shares, offsets, turn_table(), place_table()),
        (vmem,) * 4,
    )
    mine = call(
        values_kernel,
        jax.ShapeDtypeStruct((WIN, 8, 128), F32),
        (where, shares, turn_table(), place_table(), terms),
        (smem, vmem, vmem, vmem, pl.ANY),
    )
    below = lax.ppermute(mine, "z", [(k + 1, k) for k in range(PLANES - 1)])
    all_terms = lax.all_to_all(terms, "z", split_axis=0, concat_axis=0, tiled=True)
    windows, done = call(
        place_kernel,
        (jax.ShapeDtypeStruct((6, WIN * WIN * WIN), F32), jax.ShapeDtypeStruct((8, 128), F32)),
        (where, facts, mine, below),
        (smem, smem, vmem, vmem),
    )
    matrix, rhs = call(
        graph_kernel,
        (jax.ShapeDtypeStruct((64, 64), F32), jax.ShapeDtypeStruct((3, 64), F32)),
        (all_terms, graph_table(), graph_table().T.astype(ml_dtypes.bfloat16), done),
        (vmem, vmem, vmem, pl.ANY),
    )
    return windows, matrix, rhs.T


def solution(mesh):
    grid = Mesh(mesh.devices.reshape(PLANES, 2, SUBS), ("z", "core", "sub"))
    tiles = ("z", "core")
    in_specs = (P(tiles, None, "sub", None, None), P(), P(), P())
    out_specs = (P(tiles, None), P(), P())
    return jax.shard_map(local, mesh=grid, in_specs=in_specs, out_specs=out_specs, check_vma=False)
```

```python
import jax
import jax.numpy as jnp
import ml_dtypes
import numpy as np
from jax import lax
from jax.experimental import pallas as pl
from jax.experimental.pallas import tpu as pltpu
from jax.sharding import Mesh, PartitionSpec as P

REACH = 4
WIN = 9
EPSILON = 1e-06
FLOOR_SHARE = 0.05
ROW = 4
PLANES = 16
SUBS = 16
DEPTH, ACROSS, ALONG = 128, 32, 256
LOCAL = DEPTH // SUBS
HALF = ALONG // 2
VOXELS = DEPTH * ACROSS * ALONG
MAX_OFF = 5
OFFS = 2 * MAX_OFF + 1
BF = jnp.bfloat16
F32 = jnp.float32


def split_np(table):
    high = table.astype(ml_dtypes.bfloat16)
    low = (table - high.astype(np.float64)).astype(ml_dtypes.bfloat16)
    return high, low


def lane_tiles(table):
    return np.stack([table[..., :128], table[..., 128:]], axis=-3)


def angles(rows, cols, length):
    return (np.outer(rows, cols) % length) * (2.0 * np.pi / length)


def across_freq(half, sub):
    if half == 0:
        return sub
    return ACROSS // 2 if sub == 0 else ACROSS - sub


def across_table():
    table = np.zeros((2, 2, SUBS, LOCAL, LOCAL, ACROSS))
    for half in range(2):
        for sub in range(SUBS):
            theta = angles([across_freq(half, sub)], np.arange(ACROSS), ACROSS)[0]
            for plane in range(LOCAL):
                table[half, 0, sub, plane, plane] = np.cos(theta)
                table[half, 1, sub, plane, plane] = -np.sin(theta)
    return table.reshape(2, 2 * SUBS * LOCAL, LOCAL * ACROSS)


def along_table():
    table = np.zeros((2, 2, ALONG, 2, HALF))
    for half in range(2):
        theta = angles(np.arange(ALONG), np.arange(HALF) + half, ALONG)
        table[half, 0, :, 0] = np.cos(theta)
        table[half, 0, :, 1] = -np.sin(theta)
        table[half, 1, :, 0] = np.sin(theta)
        table[half, 1, :, 1] = np.cos(theta)
    return table.reshape(2, 2 * ALONG, 2 * HALF)


def extra_table():
    table = np.zeros((2, ALONG, HALF))
    table[0, :, 0] = np.where(np.arange(ALONG) % 2 == 0, 1.0, -1.0)
    table[1, :, HALF - 1] = 1.0
    return table


HALF_ROWS = 2 * SUBS * LOCAL


def plane_dft_tables():
    across, along = split_np(across_table()), split_np(along_table())
    extra = extra_table().astype(ml_dtypes.bfloat16)
    pieces = [part[half] for half in range(2) for part in across]
    pieces += [part[half] for half in range(2) for part in along]
    pieces.append(np.concatenate([extra[0], extra[1]], axis=1))
    return lane_tiles(np.concatenate(pieces, axis=0))


def wide_rows(tables, start, count):
    rows = pl.ds(pl.multiple_of(start, 256), count)
    return jnp.concatenate([tables[0, rows, :], tables[1, rows, :]], axis=1)


def across_rows(tables, half, low):
    return wide_rows(tables, (2 * half + low) * HALF_ROWS, HALF_ROWS)


def along_rows(tables, half, low):
    start = 4 * HALF_ROWS + (2 * half + low) * 2 * ALONG
    return wide_rows(tables, start, 2 * ALONG)


def extra_rows(tables, half):
    start = 4 * HALF_ROWS + 8 * ALONG
    return tables[half, start : start + ALONG, :]


def depth_table():
    theta = angles(np.arange(64), np.arange(DEPTH), DEPTH)
    cos, sin = np.cos(theta), np.sin(theta)
    sin[0] = np.where(np.arange(DEPTH) % 2 == 0, 1.0, -1.0)
    table = np.zeros((2, 2, 64, SUBS, 2, LOCAL))
    for half in range(2):
        table[0, half, :, :, half, :] = cos.reshape(64, SUBS, LOCAL)
        table[1, half, :, :, half, :] = sin.reshape(64, SUBS, LOCAL)
    return table.reshape(4 * 64, 2 * DEPTH)


ORDER = np.concatenate([np.arange(65), np.arange(127, 64, -1)])


def window_table():
    freq = np.arange(DEPTH)
    table = np.zeros((OFFS, 6, 16, DEPTH))
    low, high = (freq >= 1) & (freq < 64), freq > 64
    for index in range(OFFS):
        steps = np.arange(WIN) - REACH + index - MAX_OFF
        theta = angles(steps, freq, DEPTH)
        cos, sin = np.cos(theta), np.sin(theta)
        edge = 0.5 * cos * ((freq == 0) | (freq == 64))
        table[index, 0, :WIN] = cos
        table[index, 1, :WIN] = sin
        table[index, 2, :WIN] = cos * low + edge
        table[index, 3, :WIN] = sin * low
        table[index, 4, :WIN] = cos * high
        table[index, 5, :WIN] = edge - sin * high
    return table.reshape(OFFS, 96, DEPTH)[:, :, ORDER]


def step_table():
    step = np.arange(WIN) - REACH
    table = np.zeros((2, 2, HALF, 128))
    for half in range(2):
        theta = angles(np.arange(HALF) + half, step, ALONG)
        table[half, 0, :, :WIN] = np.cos(theta)
        table[half, 1, :, :WIN] = -np.sin(theta)
        table[half, 0, :, 64 : 64 + WIN] = np.sin(theta)
        table[half, 1, :, 64 : 64 + WIN] = np.cos(theta)
    high, low = split_np(table.reshape(2, 2 * HALF, 128) * (2.0 / VOXELS))
    return np.stack([high, low], axis=1)


def turn_table():
    step = np.arange(WIN) - REACH
    table = np.zeros((SUBS, 16, 128), np.float32)
    for sub in range(SUBS):
        theta = angles(step, [sub], ACROSS)
        table[sub, :WIN, :64] = np.cos(theta)
        table[sub, :WIN, 64:] = -np.sin(theta)
    table[0, :WIN, 64:] = np.where(step % 2 == 0, 1.0, -1.0)[:, None]
    return table


def shift_table():
    table = np.zeros((2, 2, 16, HALF))
    for half in range(2):
        theta = angles(np.arange(OFFS) - MAX_OFF, np.arange(HALF) + half, ALONG)
        table[half, 0, :OFFS] = np.cos(theta)
        table[half, 1, :OFFS] = np.sin(theta)
    return table.reshape(4, 16, HALF).astype(np.float32)


GROUP = 6


def place_table():
    table = np.zeros((3, 4, 8, 128), np.float32)
    for index in range(4 * WIN):
        pair, depth = divmod(index, WIN)
        group, row = divmod(index, GROUP)
        for along in range(WIN):
            table[:, pair, row, WIN * group + along] = (1.0, depth - REACH, along - REACH)
    return table


def circle_table():
    theta = np.arange(ACROSS) * (2.0 * np.pi / ACROSS)
    return np.stack([np.cos(theta), np.sin(theta)]).astype(np.float32)


def graph_table():
    table = np.zeros((8, PLANES, ROW * PLANES), np.float32)
    for plane in range(PLANES):
        base = ROW * plane
        pairs = [(base, base + 1), (base + 2, base + 3), (base + 1, base + 2)]
        pairs += [(base - ROW + col, base + col) for col in range(ROW)]
        for slot, (first, second) in enumerate(pairs):
            if first >= 0:
                table[slot, plane, first] = 1.0
                table[slot, plane, second] = -1.0
    return table.reshape(PLANES * 8, ROW * PLANES)


def dot(left, right):
    return jnp.dot(left, right, preferred_element_type=F32)


def split(value):
    high = value.astype(BF)
    return high, (value - high.astype(F32)).astype(BF)


def across_dft(strip, half, tables):
    both = dot(wide_rows(tables, 2 * half * HALF_ROWS, 2 * HALF_ROWS), strip)
    both = both[:HALF_ROWS] + both[HALF_ROWS:]
    rows = SUBS * LOCAL
    return jnp.concatenate([both[:rows], both[rows:]], axis=1)


def along_dft(value, half, tables, count):
    high, low = split(value)
    table_hi, table_lo = along_rows(tables, half, 0), along_rows(tables, half, 1)
    out = dot(high, table_hi) + dot(low, table_hi) + dot(high, table_lo)
    extra = extra_rows(tables, half)
    rows = SUBS * LOCAL
    edge_hi = jnp.concatenate([high[rows * k : rows * k + 16, :ALONG] for k in range(count)], axis=0)
    edge_lo = jnp.concatenate([low[rows * k : rows * k + 16, :ALONG] for k in range(count)], axis=0)
    more = dot(edge_hi, extra) + dot(edge_lo, extra)
    pieces = []
    for k in range(count):
        block = out[rows * k : rows * (k + 1)]
        head = block[:LOCAL]
        head = jnp.concatenate(
            [head[:, :HALF], head[:, HALF:] + more[16 * k : 16 * k + LOCAL]], axis=1
        )
        pieces.append(jnp.concatenate([head, block[LOCAL:]], axis=0).reshape(SUBS, LOCAL, 2 * HALF))
    return pieces


def pair_facts(where, pair_tiles, owner, pair_offset):
    plane, core = where[0], where[1]
    base = ROW * plane
    count = owner.shape[1]
    row = lax.broadcasted_iota(jnp.int32, (16, count), 0)
    place = lax.broadcasted_iota(jnp.int32, (16, count), 1)
    home = 2 * base + jnp.where(row == 1, 4, jnp.where(row == 2, 2, 0))
    up = 2 * (base - ROW + row - 3) + 1
    down = 2 * (base + 2 * core + row - 7) + 1
    wanted = jnp.where(row < 3, home, jnp.where(row < 7, up, jnp.where(row < 9, down, -100)))
    first, second = pair_tiles[0:1, :], pair_tiles[1:2, :]
    key = first * 2 + jnp.where(second - first == 1, 0, 1)
    match = wanted == key
    owned = jnp.broadcast_to(owner[...] == 2 * plane + core, match.shape)

    def total(mask, value):
        return jnp.sum(jnp.where(mask, value, 0), axis=1, keepdims=True)

    offset = [total(match, jnp.broadcast_to(pair_offset[k : k + 1, :], match.shape)) for k in range(3)]
    at = total(match, place)
    held = total(match & owned, 1)
    ordinal = total((place < at) & owned, 1)
    return offset, jnp.where(held > 0, ordinal, -1)


def chunk(pieces):
    return jnp.concatenate(pieces, axis=1).astype(BF)


def local_kernel(strips, tables, out):
    chosen = (1, 4, 2, 6)
    parts = []
    for half in range(2):
        stack = [across_dft(strips[k], half, tables) for k in chosen]
        parts.append(along_dft(jnp.concatenate(stack, axis=0), half, tables, 4))
    for k in range(4):
        out[:, 16 * k : 16 * k + 16, :] = chunk([parts[0][k], parts[1][k]])


def seam_kernel(
    where, own, other, tables, pair_tiles, owner, pair_offset, ignored, out, facts, offsets
):
    del ignored
    offset, slot = pair_facts(where, pair_tiles, owner, pair_offset)
    lane = lax.broadcasted_iota(jnp.int32, (16, 128), 1)
    facts[...] = jnp.where(
        lane == 0, offset[0], jnp.where(lane == 1, offset[1], jnp.where(lane == 2, offset[2], slot))
    )
    lane = lane[:8]
    offsets[...] = jnp.where(
        lane == 1, offset[0][:8], jnp.where(lane == 2, offset[1][:8], offset[2][:8])
    ).astype(F32)
    core = where[1]
    mine, theirs = own[...], other[...]
    first = jnp.where(core == 0, mine, theirs)
    second = jnp.where(core == 0, theirs, mine)
    stack = [across_dft(strip, core, tables) for strip in (first, second)]
    out[...] = chunk(along_dft(jnp.concatenate(stack, axis=0), core, tables, 2))


def remote_kernel(here, seam, below, tables, out, moved):
    kept = [
        pltpu.make_async_copy(here, out.at[:, pl.ds(0, 64), :], moved.at[0]),
        pltpu.make_async_copy(seam, out.at[:, pl.ds(96, 16), :], moved.at[1]),
    ]
    for copy in kept:
        copy.start()
    parts = []
    for half in range(2):
        stack = [across_dft(below[k], half, tables) for k in range(2)]
        parts.append(along_dft(jnp.concatenate(stack, axis=0), half, tables, 2))
    for k in range(2):
        out[:, 64 + 16 * k : 80 + 16 * k, :] = chunk([parts[0][k], parts[1][k]])
    for copy in kept:
        copy.wait()


def spectrum_of(block, zeroth, held, depth_both):
    both = dot(depth_both, block)
    both = both[:256] + both[256:]
    cos, sin = both[:DEPTH], both[DEPTH:]
    cos_re, cos_im = cos[:, :HALF], cos[:, HALF:]
    sin_re, sin_im = sin[:, :HALF], sin[:, HALF:]
    low_re = jnp.where(zeroth | held, cos_re, cos_re + sin_im)
    low_im = jnp.where(zeroth, cos_im, jnp.where(held, 0.0, cos_im) - sin_re)
    high_re = jnp.where(zeroth, sin_re, jnp.where(held, cos_im, cos_re - sin_im))
    high_im = jnp.where(zeroth, sin_im, jnp.where(held, sin_im, cos_im + sin_re))

    def rows(low, high):
        return jnp.concatenate([low[:64], high[:64], low[64:], high[64:]], axis=0)

    return rows(low_re, high_re), rows(low_im, high_im)


def phase_of(first, second, edge):
    floor = (FLOOR_SHARE * VOXELS) ** 2
    first_re, first_im = first
    second_re, second_im = second
    straight, crossed = first_re * second_re, first_im * second_im
    imag = first_im * second_re - first_re * second_im
    if edge is None:
        real = straight + crossed
        norm = lax.rsqrt(real * real + imag * imag + floor)
        return real * norm, imag * norm
    real = straight + jnp.where(edge, 0.0, crossed)
    imag = jnp.where(edge, crossed, imag)
    real_sq, imag_sq = real * real, imag * imag
    norm = lax.rsqrt(real_sq + jnp.where(edge, 0.0, imag_sq) + floor)
    norm_im = jnp.where(edge, lax.rsqrt(imag_sq + floor), norm)
    return real * norm, imag * norm_im


def window_kernel(where, meta, circle, got, depth, vhi, vlo, steps, shift, out):
    c, d = where[1], where[2]
    row = lax.broadcasted_iota(jnp.int32, (DEPTH, HALF), 0)
    lane = lax.broadcasted_iota(jnp.int32, (DEPTH, HALF), 1)
    zeroth = lax.rem(row, 64) == 0
    nowhere = jnp.where(d == 0, 0, 2 * HALF)

    def special(half_of_row):
        return (lane == half_of_row * (HALF - 1) + nowhere) & (lax.rem(row, 64) != 0)

    def edges(count, half_of_row):
        row = lax.broadcasted_iota(jnp.int32, (count, HALF), 0)
        lane = lax.broadcasted_iota(jnp.int32, (count, HALF), 1)
        return (lane == half_of_row(row) * (HALF - 1) + nowhere) & (lax.rem(row, 64) == 0)

    held = special(row // 64)
    edge = edges(2 * DEPTH, lambda row: row // DEPTH)
    depth_both = wide_rows(depth, 0, 512)

    def spectrum(slot, held):
        block = got[:, 16 * slot : 16 * slot + 16, :].reshape(2 * DEPTH, 2 * HALF)
        return spectrum_of(block, zeroth, held, depth_both)

    small_lane = lax.broadcasted_iota(jnp.int32, (16, HALF), 1)

    def window_rows(phase, half, slot):
        off_z, off_y, off_x = meta[slot, 0], meta[slot, 1], meta[slot, 2]
        high, low = split(jnp.concatenate(phase, axis=1))
        table_hi, table_lo = vhi[off_z + MAX_OFF], vlo[off_z + MAX_OFF]
        rows = dot(jnp.concatenate([table_hi, table_lo], axis=0), high)
        rows = rows[:96] + rows[96:] + dot(table_hi, low)
        part = [(rows[16 * k : 16 * k + 16, :HALF], rows[16 * k : 16 * k + 16, HALF:]) for k in range(6)]
        held = small_lane == half * (HALF - 1) + nowhere
        real = jnp.where(held, part[2][0] - part[3][1], part[0][0] - part[1][1])
        imag = jnp.where(held, 0.0, part[1][0] + part[0][1])
        freq_y = jnp.where(half == 0, d, jnp.where(d == 0, ACROSS // 2, ACROSS - d))
        turn = lax.rem(freq_y * (off_y + ACROSS), ACROSS)
        cos_y, sin_y = circle[0, turn], circle[1, turn]
        cos_x = shift[2 * half, pl.ds(off_x + MAX_OFF, 1), :]
        sin_x = shift[2 * half + 1, pl.ds(off_x + MAX_OFF, 1), :]
        cos = cos_x * cos_y - sin_x * sin_y
        sin = sin_x * cos_y + cos_x * sin_y
        turned = jnp.concatenate([real * cos - imag * sin, real * sin + imag * cos], axis=1)
        other = jnp.sum(jnp.where(held, part[4][0] + part[5][1], 0.0), axis=1, keepdims=True)
        even = (lax.rem(small_lane + off_x + 6, 2) == 0) | (half == 1)
        sign = jnp.where(even, 1.0, -1.0) * (cos_y * (2.0 / VOXELS))
        return turned, other * jnp.where(small_lane < WIN, sign, 0.0)

    terms, extra = ([], []), ([], [])
    for first, second, slot in ((0, 1, c), (4, 2, 3 + 2 * c), (5, 3, 4 + 2 * c)):
        real, imag = phase_of(spectrum(first, held), spectrum(second, held), edge)
        for half in range(2):
            rows = slice(DEPTH * half, DEPTH * (half + 1))
            turned, more = window_rows((real[rows], imag[rows]), half, slot)
            terms[half].append(turned)
            extra[half].append(more)
    real, imag = spectrum(6, special(c))
    seam_edge = edges(DEPTH, lambda row: c)
    phase = phase_of((real[:DEPTH], imag[:DEPTH]), (real[DEPTH:], imag[DEPTH:]), seam_edge)
    turned, more = window_rows(phase, c, 2)
    for half in range(2):
        terms[half].append(jnp.where(c == half, turned, 0.0))
        extra[half].append(jnp.where(c == half, more, 0.0))
    sums = []
    for half in range(2):
        high, low = split(jnp.concatenate(terms[half], axis=0))
        table_hi, table_lo = steps[half, 0], steps[half, 1]
        total = dot(high, table_hi) + dot(low, table_hi) + dot(high, table_lo)
        sums.append(total + jnp.concatenate(extra[half], axis=0))
    lane = lax.broadcasted_iota(jnp.int32, sums[0].shape, 1)
    both = sums[0] + jnp.where(lane < 64, sums[1], -sums[1])
    apart = jnp.where(lane < 64, sums[0], pltpu.roll(sums[1], 64, 1))
    both = jnp.where(d == 0, apart, both)
    rows = jnp.concatenate([both[16 * k : 16 * k + WIN] for k in range(4)], axis=0)
    packed = rows[:GROUP]
    for group in range(1, GROUP):
        packed = packed + pltpu.roll(rows[GROUP * group : GROUP * (group + 1)], WIN * group, 1)
    packed = jnp.concatenate([packed, jnp.zeros((2, 128), F32)], axis=0)
    out[...] = jnp.broadcast_to(packed[None], out.shape)


def across_sums(got, turns):
    sums = [[None] * WIN, [None] * WIN]
    for sub in range(SUBS):
        turn = turns[sub]
        for core in range(2):
            value = got[SUBS * core + sub]
            for step in range(WIN):
                term = value * turn[step : step + 1]
                sums[core][step] = term if sub == 0 else sums[core][step] + term
    sums = [[value + pltpu.roll(value, 64, 1) for value in side] for side in sums]
    return sums, [left + right for left, right in zip(*sums)]


def energy_kernel(got, offsets, turns, places, terms):
    sums, seam = across_sums(got, turns)
    totals = []
    for side in (sums[0], sums[1], seam):
        squares = [value * value for value in side]
        total = squares[0]
        for value in squares[1:]:
            total = total + value
        across = squares[0] * float(-REACH)
        for step in range(1, WIN):
            across = across + squares[step] * float(step - REACH)
        totals.append((total, across))
    slots = ((0, 0), (1, 0), (2, 3), (0, 1), (0, 2), (1, 1), (1, 2))

    def stacked(kind, which):
        rows = [
            jnp.sum(totals[side][which] * places[kind, pair], axis=0, keepdims=True)
            for side, pair in slots
        ]
        rows = jnp.concatenate(rows + [jnp.zeros((1, 128), F32)], axis=0)
        return jnp.sum(rows, axis=1, keepdims=True)

    energy = stacked(0, 0)
    moments = [stacked(1, 0), stacked(0, 1), stacked(2, 0)]
    lane = lax.broadcasted_iota(jnp.int32, (8, 128), 1)
    mixed = jnp.where(lane == 1, moments[0], jnp.where(lane == 2, moments[1], moments[2]))
    place = offsets[...] + mixed / (energy + EPSILON)
    value = jnp.where(lane == 0, energy, energy * place)
    value = jnp.where(lane < 4, value, 0.0)
    line = value[0:1]
    for slot in range(1, 7):
        line = line + pltpu.roll(value[slot : slot + 1], 4 * slot, 1)
    terms[...] = jnp.broadcast_to(line[None], terms.shape)


def values_kernel(where, got, turns, places, ignored, windows):
    del ignored
    sums, seam = across_sums(got, turns)
    is_left = where[1] == 0
    at_seam = places[0, 3] > 0.0
    for step in range(WIN):
        mine = jnp.where(is_left, sums[0][step], sums[1][step])
        windows[step] = jnp.where(at_seam, seam[step], mine)


def unpack(packed):
    lane = lax.broadcasted_iota(jnp.int32, (8, 128), 1)
    values = [packed[step] for step in range(WIN)]
    groups = []
    for group in range(GROUP):
        inside = (lane >= WIN * group) & (lane < WIN * (group + 1))
        rows = jnp.zeros((8, 128), F32)
        for step in range(WIN):
            moved = WIN * (step - group) % 128
            value = jnp.where(inside, values[step], 0.0)
            rows = rows + (pltpu.roll(value, moved, 1) if moved else value)
        groups.append(rows[:GROUP])
    rows = jnp.concatenate(groups, axis=0)
    return [rows[WIN * pair : WIN * (pair + 1)] for pair in range(4)]


def graph_kernel(terms, graph, turned, ignored, matrix, rhs):
    del ignored
    lines = jnp.concatenate([terms[plane, 0:1] for plane in range(PLANES)], axis=0)
    slots = [lines] + [pltpu.roll(lines, 128 - 4 * slot, 1) for slot in range(1, 8)]
    value = jnp.concatenate(slots, axis=0)
    wide = jnp.concatenate([graph[...] * value[:, :1], value[:, :64]], axis=1)
    high, rest = wide.astype(BF), wide - wide.astype(BF).astype(F32)
    middle, low = split(rest)
    table = turned[...]
    both = dot(table, high) + dot(table, middle) + dot(table, low)
    matrix[...] = both[:, :64]
    rhs[...] = both.T[65:68]


def place_kernel(where, meta, mine, below, windows, done):
    done[...] = mine[0]
    c = where[1]
    slot = lax.broadcasted_iota(jnp.int32, (6, 128), 0)
    blocks = unpack(mine) + unpack(below)[1:3]
    places = [slot == meta[k, 3] for k in (c, 3 + 2 * c, 4 + 2 * c, 2, 7, 8)]
    for step in range(WIN):
        rows = jnp.zeros((6, 128), F32)
        for block, place in zip(blocks, places):
            rows = jnp.where(place, block[step : step + 1], rows)
        windows[:, WIN * WIN * step : WIN * WIN * (step + 1)] = rows[:, : WIN * WIN]


def call(kernel, shapes, operands, spaces, **params):
    specs = [pl.BlockSpec(memory_space=space) for space in spaces]
    outs = jax.tree.map(lambda _: pl.BlockSpec(memory_space=pltpu.VMEM), shapes)
    return pl.pallas_call(
        kernel,
        out_shape=shapes,
        in_specs=specs,
        out_specs=outs,
        compiler_params=pltpu.CompilerParams(vmem_limit_bytes=16 * 1024 * 1024),
        **params,
    )(*operands)


def local(strips, pair_tiles, pair_owner, pair_offset):
    where = jnp.stack([lax.axis_index(name) for name in ("z", "core", "sub")]).astype(jnp.int32)
    tables = plane_dft_tables()
    depth = lane_tiles(np.concatenate(split_np(depth_table()), axis=0))
    vhi, vlo = split_np(window_table())
    vmem, smem = pltpu.VMEM, pltpu.SMEM

    tiles = strips.reshape(8, LOCAL * ACROSS, ALONG)
    bottoms = jnp.stack([tiles[3], tiles[7]])
    from_above = lax.ppermute(bottoms, "z", [(k, k + 1) for k in range(PLANES - 1)])
    core, bottoms = lax.optimization_barrier((where[1], bottoms))
    own = lax.dynamic_index_in_dim(tiles, 5 - 5 * core, 0, keepdims=False)
    other = lax.ppermute(own, "core", [(0, 1), (1, 0)])

    here = call(
        local_kernel, jax.ShapeDtypeStruct((SUBS, 64, 2 * HALF), BF), (tiles, tables), (vmem, vmem)
    )
    seam, facts, offsets = call(
        seam_kernel,
        (
            jax.ShapeDtypeStruct((SUBS, 16, 2 * HALF), BF),
            jax.ShapeDtypeStruct((16, 128), jnp.int32),
            jax.ShapeDtypeStruct((8, 128), F32),
        ),
        (
            where, own, other, tables,
            pair_tiles.T, pair_owner.reshape(1, -1), pair_offset.T, here,
        ),
        (smem,) + (vmem,) * 6 + (pl.ANY,),
    )
    sent = call(
        remote_kernel,
        jax.ShapeDtypeStruct((SUBS, 112, 2 * HALF), BF),
        (here, seam, from_above, tables),
        (vmem,) * 4,
        scratch_shapes=[pltpu.SemaphoreType.DMA((2,))],
    )
    got = lax.all_to_all(sent, "sub", split_axis=0, concat_axis=0, tiled=True)
    partial = call(
        window_kernel,
        jax.ShapeDtypeStruct((2 * SUBS, 8, 128), F32),
        (where, facts, circle_table(), got, depth, vhi, vlo, step_table(), shift_table()),
        (smem,) * 3 + (vmem,) * 6,
    )
    shares = lax.all_to_all(partial, ("core", "sub"), split_axis=0, concat_axis=0, tiled=True)
    terms = call(
        energy_kernel,
        jax.ShapeDtypeStruct((PLANES, 8, 128), F32),
        (shares, offsets, turn_table(), place_table()),
        (vmem,) * 4,
    )
    mine = call(
        values_kernel,
        jax.ShapeDtypeStruct((WIN, 8, 128), F32),
        (where, shares, turn_table(), place_table(), terms),
        (smem, vmem, vmem, vmem, pl.ANY),
    )
    below = lax.ppermute(mine, "z", [(k + 1, k) for k in range(PLANES - 1)])
    all_terms = lax.all_to_all(terms, "z", split_axis=0, concat_axis=0, tiled=True)
    windows, done = call(
        place_kernel,
        (jax.ShapeDtypeStruct((6, WIN * WIN * WIN), F32), jax.ShapeDtypeStruct((8, 128), F32)),
        (where, facts, mine, below),
        (smem, smem, vmem, vmem),
    )
    matrix, rhs = call(
        graph_kernel,
        (jax.ShapeDtypeStruct((64, 64), F32), jax.ShapeDtypeStruct((3, 64), F32)),
        (all_terms, graph_table(), graph_table().T.astype(ml_dtypes.bfloat16), done),
        (vmem, vmem, vmem, pl.ANY),
    )
    return windows, matrix, rhs.T


def solution(mesh):
    grid = Mesh(mesh.devices.reshape(PLANES, 2, SUBS), ("z", "core", "sub"))
    tiles = ("z", "core")
    in_specs = (P(tiles, None, "sub", None, None), P(), P(), P())
    out_specs = (P(tiles, None), P(), P())
    return jax.shard_map(local, mesh=grid, in_specs=in_specs, out_specs=out_specs, check_vma=False)
```
